32 devices in a mesh: dp: 16 (over z, y, x), mp: 2 (over core).
Axes of the slice: x: 2, y: 2, z: 4, core: 2. Of those that a mesh axis runs over, the one named last changes fastest.
Arguments:
- query_states: bfloat16 [512, 4096], P('dp')
- passage_states: bfloat16 [4096, 4096], P('dp')
- head_weight: bfloat16 [4096, 2048], P(None, 'mp'), may hold values from -0.09375 to 0.09375
- positives: int32 [512], P('dp'), may hold values from 0 to 4095, as said below
- negatives: int32 [512, 8], P('dp'), may hold values from 0 to 4095, as said below
- search_cost_incoming_slope: float32 [512], P('dp'), may hold values from 20 to 200
Outputs:
- losses: float32 [512], P('dp')
- query_grads: bfloat16 [512, 4096], P('dp', 'mp')
- passage_grads: bfloat16 [4096, 4096], P('dp', 'mp')
The draws below stay inside these ranges and needn't reach their ends.
Inputs may be any that keep to these rules, and one draw needn't show every extreme that they name: `positives`: the queries of one aligned block of 32 rows name, over their positive and hard negatives together, at most 36 passages of any one aligned block of 256 passages (repeats counted); in every draw one block of passages is named exactly 36 times by the queries of every block. `negatives`: see positives: the bound counts both arguments together.
All inputs are finite; a program needn't handle non-finite values.
Results may differ from the reference program's by a relative error of at most 0.015.
Values may be sent and summed in bfloat16 or wider, within the bound.
A program may use at most 128 MiB of HBM per device.

```python
import math
import jax
import jax.numpy as jnp
from jax import lax

D = 4096
E = 2048
NEG = 8
Q_DEV = 32
P_DEV = 256
QUERIES = 512
PASSAGES = 4096
PASSAGE_LIMIT = 36
N_DP = 16


passage_common = 0.65


query_common = 2.86


query_noise = 3.8


def passage_lists(key):
    key = jax.random.fold_in(key, 11)
    rank_key, pick_key, row_key, order_key = jax.random.split(key, 4)
    owner_ranks = jax.random.permutation(rank_key, N_DP)
    popular_count = max(1, N_DP // 16)
    requests = Q_DEV * (NEG + 1)
    slot_owner = jnp.arange(N_DP * PASSAGE_LIMIT) // PASSAGE_LIMIT
    entry_ranking = owner_ranks[slot_owner]
    holder_offset = jnp.where(entry_ranking == 0, -4 * N_DP * PASSAGE_LIMIT, jnp.where(entry_ranking < popular_count, -2 * N_DP * PASSAGE_LIMIT, 0))

    def one_device(device_random_key):
        entry_logits = jax.random.permutation(device_random_key, N_DP * PASSAGE_LIMIT) + holder_offset
        chosen = jnp.argsort(entry_logits, stable=True)[:requests]
        return slot_owner[chosen]
    owners = jax.vmap(one_device)(jax.random.split(pick_key, N_DP))
    local_rows = jax.random.randint(row_key, (N_DP, requests), 0, P_DEV)
    shuffled = jax.vmap(lambda sub_key: jax.random.permutation(sub_key, requests))(jax.random.split(order_key, N_DP))
    passage_ids = jnp.take_along_axis(owners * P_DEV + local_rows, shuffled, axis=1)
    return passage_ids.reshape(QUERIES, NEG + 1).astype(jnp.int32)


def shared_parts(key):
    identity_key = jax.random.fold_in(key, 41)
    common_row = jax.random.normal(jax.random.fold_in(key, 43), (1, D), jnp.float32)
    column_scale = jnp.exp(jax.random.uniform(jax.random.fold_in(key, 31), (1, D), jnp.float32, math.log(0.5), math.log(2.0)))
    return (identity_key, common_row, column_scale)


def identity_rows(identity_key, passage_ids):
    return jax.vmap(lambda passage_id: jax.random.normal(jax.random.fold_in(identity_key, passage_id), (D,), jnp.float32))(passage_ids)


def row_scales(key, count, spread):
    return jnp.exp(jax.random.uniform(key, (count, 1), jnp.float32, 0.0, math.log(spread)))


def draw_positives(key, part):
    return passage_lists(key)[:, 0]


def draw_negatives(key, part):
    return passage_lists(key)[:, 1:]


def draw_query_states(key, part):
    passage_ids = passage_lists(key)
    identity_key, common_row, column_scale = shared_parts(key)
    partner_key = jax.random.fold_in(key, 9)
    key = jax.random.fold_in(key, 5)
    weight_key, ratio_key, noise_key, scale_key = jax.random.split(key, 4)
    leading = jnp.exp(jax.random.uniform(weight_key, (QUERIES, 1), jnp.float32, math.log(0.8), math.log(1.25)))
    ratios = jax.random.uniform(ratio_key, (QUERIES, NEG + 1), jnp.float32, 0.55, 0.8)
    first_column = jnp.arange(NEG + 1)[None, :] == 0
    ratios = jnp.where(first_column, 1.0, ratios)
    signal = jnp.zeros((QUERIES, D), jnp.float32) + query_common * common_row
    for column in range(NEG + 1):
        signal = signal + leading * ratios[:, column:column + 1] * identity_rows(identity_key, passage_ids[:, column])
    partner_ids = jnp.roll(passage_ids[:, 0], -(QUERIES // 2))
    partner_ratio = jax.random.uniform(partner_key, (QUERIES, 1), jnp.float32, 0.55, 0.8)
    signal = signal + leading * partner_ratio * identity_rows(identity_key, partner_ids)
    noise_part = jax.random.normal(noise_key, (QUERIES, D), jnp.float32)
    row_scale = row_scales(scale_key, QUERIES, 10.0)
    return ((signal + query_noise * noise_part) * row_scale * column_scale).astype(jnp.bfloat16)


def draw_passage_states(key, part):
    identity_key, common_row, column_scale = shared_parts(key)
    key = jax.random.fold_in(key, 7)
    identities = identity_rows(identity_key, jnp.arange(PASSAGES))
    row_scale = row_scales(key, PASSAGES, 10.0)
    return ((identities + passage_common * common_row) * row_scale * column_scale).astype(jnp.bfloat16)


def level_of(key, shape, pieces, low, largest):
    def one(axis_at, shards_of):
        draws = jax.random.uniform(jax.random.fold_in(jax.random.fold_in(key, 6), axis_at), (shards_of,), jnp.float32, low / len(pieces), largest / len(pieces))
        return jnp.repeat(jnp.exp(draws), shape[axis_at] // shards_of).reshape((-1,) + (1,) * (len(shape) - axis_at - 1))

    level = one(*pieces[0])
    for cut in pieces[1:]:
        level = level * one(*cut)
    return level


def centred(own_key, shape, scale, reach, pieces=(), dtype=jnp.bfloat16):
    loudness = level_of(own_key, shape, pieces, -0.22, 0.18) if pieces else 1.0
    entries = jax.random.normal(own_key, shape, jnp.float32) * scale * loudness
    return jnp.minimum(jnp.maximum(entries, -reach), reach).astype(dtype)


def setup_inputs(seed: int = 0) -> dict:
    streams_of = jax.random.split(jax.random.key(seed), 7)
    query_states = draw_query_states(jax.random.fold_in(streams_of[6], 71), 0)
    passage_states = draw_passage_states(jax.random.fold_in(streams_of[6], 71), 0)
    head_weight = centred(streams_of[2], (D, E), D ** -0.5, 0.09375, ((1, 2),))
    positives = draw_positives(jax.random.fold_in(streams_of[6], 71), 0)
    negatives = draw_negatives(jax.random.fold_in(streams_of[6], 71), 0)
    search_cost_incoming_slope = jnp.clip(jnp.exp(math.log(200.0) - 2.3025851 * jax.random.uniform(streams_of[5], (QUERIES,), jnp.float32) ** level_of(streams_of[5], (QUERIES,), ((0, 16),), -0.2, 0.2)), 20.0, 200.0)
    return dict(query_states=query_states, passage_states=passage_states, head_weight=head_weight, positives=positives, negatives=negatives, search_cost_incoming_slope=search_cost_incoming_slope)


sharpness_divisor = 0.02

def normalize(states, weight):
    projected = jnp.dot(states, weight, preferred_element_type=jnp.float32)
    inv_norm = lax.rsqrt(lax.optimization_barrier(jnp.sum(projected * projected, axis=1, keepdims=True)) + 1e-06)
    return (projected * inv_norm, inv_norm)

def tangent(unit_rows, inv_norm, upstream):
    radial = lax.optimization_barrier(jnp.sum(unit_rows * upstream, axis=1, keepdims=True))
    return (inv_norm * (upstream - unit_rows * radial)).astype(jnp.bfloat16)

def reference(query_states, passage_states, head_weight, positives, negatives, search_cost_incoming_slope):
    q_unit, q_inv = normalize(query_states, head_weight)
    p_unit, p_inv = normalize(passage_states, head_weight)
    search_embedding_matrix = q_unit.astype(jnp.bfloat16)
    p_embed = p_unit.astype(jnp.bfloat16)
    matching_document_matrix = p_embed[positives]
    distractor_embedding_matrix = p_embed[negatives]
    sibling_document_similarity = jnp.dot(search_embedding_matrix, matching_document_matrix.T, preferred_element_type=jnp.float32) / sharpness_divisor
    fetched_distractor_similarity = jnp.einsum('bm,bgm->bg', search_embedding_matrix.astype(jnp.float32), distractor_embedding_matrix.astype(jnp.float32), precision=lax.Precision.HIGHEST) / sharpness_divisor
    log_total = jnp.log(lax.optimization_barrier(jnp.sum(jnp.exp(sibling_document_similarity), axis=1)) + lax.optimization_barrier(jnp.sum(jnp.exp(fetched_distractor_similarity), axis=1)))
    losses = log_total - jnp.diagonal(sibling_document_similarity)
    indices = jnp.arange(QUERIES)
    self_match_filter = (indices[:, None] == indices[None, :]).astype(jnp.float32)
    sibling_document_likelihood = jnp.exp(sibling_document_similarity - log_total[:, None])
    fetched_distractor_likelihood = jnp.exp(fetched_distractor_similarity - log_total[:, None])
    sibling_document_slope = (search_cost_incoming_slope[:, None] * (sibling_document_likelihood - self_match_filter) / sharpness_divisor).astype(jnp.bfloat16)
    fetched_distractor_slope = search_cost_incoming_slope[:, None] * fetched_distractor_likelihood / sharpness_divisor
    q_grad = jnp.dot(sibling_document_slope, matching_document_matrix, preferred_element_type=jnp.float32)
    q_grad = q_grad + jnp.einsum('qk,qke->qe', fetched_distractor_slope, distractor_embedding_matrix.astype(jnp.float32), precision=lax.Precision.HIGHEST)
    pos_grad = lax.dot_general(sibling_document_slope, search_embedding_matrix, (((0,), (0,)), ((), ())), preferred_element_type=jnp.float32)
    neg_grad = fetched_distractor_slope[:, :, None] * search_embedding_matrix.astype(jnp.float32)[:, None, :]
    p_grad = jnp.zeros((PASSAGES, E), jnp.float32)
    p_grad = p_grad.at[positives].add(pos_grad)
    p_grad = p_grad.at[negatives.reshape(-1)].add(neg_grad.reshape(-1, E))
    q_dir = tangent(q_unit, q_inv, q_grad)
    p_dir = tangent(p_unit, p_inv, p_grad)
    dims = (((1,), (1,)), ((), ()))
    query_grads = lax.dot_general(q_dir, head_weight, dims, preferred_element_type=jnp.float32).astype(jnp.bfloat16)
    passage_grads = lax.dot_general(p_dir, head_weight, dims, preferred_element_type=jnp.float32).astype(jnp.bfloat16)
    return (losses, query_grads, passage_grads)
```

```python
import jax
import jax.numpy as jnp
from jax import lax
from jax.sharding import PartitionSpec as P

temperature = 0.02
rows_by_rows = (((1,), (1,)), ((), ()))
first_by_first = (((0,), (0,)), ((), ()))


def per_device(
    query_states, passage_states, head_weight, positives, negatives, search_cost_incoming_slope
):
    q_rows = query_states.shape[0]
    p_rows = passage_states.shape[0]
    half = head_weight.shape[0] // 2
    position = lax.axis_index("dp")
    core = lax.axis_index("mp")
    swap = [(0, 1), (1, 0)]

    lists = jnp.concatenate(
        [
            positives[:, None].astype(jnp.float32),
            negatives.astype(jnp.float32),
            search_cost_incoming_slope[:, None],
        ],
        axis=1,
    )
    all_lists = lax.all_gather(lists, "dp", axis=0, tiled=True)

    q_proj = jnp.dot(query_states, head_weight, preferred_element_type=jnp.float32)
    q_half = lax.all_gather(q_proj.astype(jnp.bfloat16), "dp", axis=0, tiled=True)
    p_proj = jnp.dot(passage_states, head_weight, preferred_element_type=jnp.float32)
    p_half = p_proj.astype(jnp.bfloat16)
    p_square = jnp.sum(p_proj * p_proj, axis=1)
    q_square = jnp.sum(jnp.square(q_half.astype(jnp.float32)), axis=1)
    raw = lax.dot_general(q_half, p_half, rows_by_rows, preferred_element_type=jnp.float32)
    raw, p_square, q_square = [
        x + lax.ppermute(x, "mp", swap) for x in (raw, p_square, q_square)
    ]
    p_inv = lax.rsqrt(p_square + 1e-06)
    q_inv = lax.rsqrt(q_square + 1e-06)
    scores = raw * (q_inv[:, None] * (1.0 / temperature)) * p_inv[None, :]

    numbers = (position * p_rows + jnp.arange(p_rows)).astype(jnp.float32)
    own = (all_lists[:, :1] == numbers[None, :]).astype(jnp.float32)
    weight = jnp.sum(own, axis=0)[None, :]
    for k in range(negatives.shape[1]):
        weight = weight + (all_lists[:, k + 1 : k + 2] == numbers[None, :]).astype(jnp.float32)
    powers = weight * jnp.exp(scores)
    sums = jnp.stack(
        [
            jnp.sum(powers, axis=1),
            jnp.sum(powers * scores, axis=1),
            jnp.sum(own * scores, axis=1),
        ]
    )
    total, moment, hit = lax.psum(sums, "dp")
    slope = all_lists[:, -1]
    grads = (slope * (1.0 / temperature))[:, None] * (
        powers * (1.0 / total)[:, None] - own
    )

    q_part = jnp.dot(
        (grads * p_inv[None, :]).astype(jnp.bfloat16), p_half, preferred_element_type=jnp.float32
    )
    q_grad = lax.psum_scatter(q_part, "dp", scatter_dimension=0, tiled=True)

    p_grad = lax.dot_general(
        (grads * q_inv[:, None]).astype(jnp.bfloat16),
        q_half,
        first_by_first,
        preferred_element_type=jnp.float32,
    )
    p_radial = temperature * jnp.sum(grads * scores, axis=0)
    p_dir = p_inv[:, None] * (p_grad - p_proj * (p_inv * p_radial)[:, None])

    mine = lambda x: lax.dynamic_slice_in_dim(x, position * q_rows, q_rows, 0)
    total, moment, hit, slope, q_inv = [mine(x) for x in (total, moment, hit, slope, q_inv)]
    losses = jnp.log(total) - hit
    q_radial = slope * (moment / total - hit)
    q_dir = q_inv[:, None] * (q_grad - q_proj * (q_inv * q_radial)[:, None])

    near = lax.dynamic_slice_in_dim(head_weight, core * half, half, 0)
    far = lax.dynamic_slice_in_dim(head_weight, (1 - core) * half, half, 0)

    def back(rows):
        rows = rows.astype(jnp.bfloat16)
        sent = lax.dot_general(rows, far, rows_by_rows, preferred_element_type=jnp.float32)
        got = lax.ppermute(sent.astype(jnp.bfloat16), "mp", swap)
        kept = lax.dot_general(rows, near, rows_by_rows, preferred_element_type=jnp.float32)
        return (kept + got.astype(jnp.float32)).astype(jnp.bfloat16)

    return losses, back(q_dir), back(p_dir)


def solution(mesh):
    placed = (P("dp", None), P("dp", None), P(None, "mp"), P("dp"), P("dp", None), P("dp"))
    return jax.shard_map(
        per_device,
        mesh=mesh,
        in_specs=placed,
        out_specs=(P("dp"), P("dp", "mp"), P("dp", "mp")),
        check_vma=False,
    )
```

```python
import functools

import jax
import jax.numpy as jnp
from jax import lax
from jax.experimental import pallas as pl
from jax.experimental.pallas import tpu as pltpu
from jax.sharding import PartitionSpec as P

temperature = 0.02
by_rows = (((1,), (1,)), ((), ()))
by_first = (((0,), (0,)), ((), ()))
f32 = jnp.float32
bf16 = jnp.bfloat16
tile = 128
w_parts = 8
strip = 32


def dot(x, y, dims=(((1,), (0,)), ((), ()))):
    return lax.dot_general(x, y, dims, preferred_element_type=f32)


def remote(src, dst, send, recv, where):
    return pltpu.make_async_remote_copy(
        src_ref=src,
        dst_ref=dst,
        send_sem=send,
        recv_sem=recv,
        device_id=where,
        device_id_type=pl.DeviceIdType.MESH,
    )


def kernel(
    n,
    names,
    q_hbm,
    p_hbm,
    w_hbm,
    lists_ref,
    loss_ref,
    q_out,
    p_out,
    qs,
    ps,
    w,
    q_proj,
    q_all,
    p_proj,
    p_half,
    p_dir,
    slots,
    lists,
    psq,
    psq_far,
    col,
    raw,
    raw_far,
    g_q,
    g_p,
    t_slots,
    mh,
    mh_slots,
    turn,
    part,
    r1,
    r2,
    r3,
    q_grad,
    p_send,
    p_recv,
    q_send,
    q_recv,
    load,
    pair,
    z_sem,
    x_sem,
    y_sem,
    fx_sem,
    fy_sem,
    list_sem,
    t_sem,
    mh_sem,
    s1_sem,
    s2_sem,
    s3_sem,
    back_sem,
):
    rows, depth = qs.shape
    p_rows, width = p_proj.shape
    queries = q_all.shape[0]
    piece = rows // 2
    group = tile // rows
    na = n // group
    half = depth // 2
    me = lax.axis_index("dp")
    core = lax.axis_index("mp")
    a, b = me // group, lax.rem(me, group)
    x, y = lax.rem(me, 2), lax.rem(me // 2, 2)
    dx, dy = 1 - 2 * x, 2 - 4 * y
    xp, yp, other = {"dp": me + dx}, {"dp": me + dy}, {"mp": 1 - core}

    k_rows = depth // w_parts

    def w_load(i):
        at = pl.ds(pl.multiple_of(i * k_rows, k_rows), k_rows)
        return pltpu.make_async_copy(w_hbm.at[at, :], w.at[at, :], load.at[i])

    q_load = pltpu.make_async_copy(q_hbm, qs, load.at[w_parts])
    p_load = pltpu.make_async_copy(p_hbm, ps, load.at[w_parts + 1])
    q_load.start()
    for i in range(w_parts):
        w_load(i).start()
    p_load.start()

    barrier = pltpu.get_barrier_semaphore()

    @pl.loop(1, n)
    def _(k):
        pl.semaphore_signal(
            barrier,
            inc=1,
            device_id={"dp": lax.rem(me + k, n)},
            device_id_type=pl.DeviceIdType.MESH,
        )

    pl.semaphore_signal(
        barrier, inc=1, device_id=other, device_id_type=pl.DeviceIdType.MESH
    )

    q_load.wait()
    q_proj[...] = jnp.zeros_like(q_proj)

    @pl.loop(0, w_parts)
    def _(i):
        w_load(i).wait()
        at = pl.ds(pl.multiple_of(i * k_rows, k_rows), k_rows)
        q_proj[...] += dot(qs[:, at], w[at, :])

    def block(i):
        return q_all.at[pl.ds(pl.multiple_of(i * rows, rows), rows), :]

    def bit(ref, i, h):
        return ref.at[pl.ds(pl.multiple_of(i * rows + h * piece, piece), piece), :]

    q_all[pl.ds(pl.multiple_of(me * rows, rows), rows), :] = q_proj[...].astype(bf16)
    pl.semaphore_wait(barrier, n)

    def z_copy(s, i):
        to = {"dp": lax.rem(a + s, na) * group + b}
        return remote(block(i), block(i), z_sem.at[0, s], z_sem.at[1, s], to)

    def column(s):
        return lax.rem(a - s + na, na) * group + b

    def x_copy(s, i):
        return remote(block(i), block(i), x_sem.at[0, s], x_sem.at[1, s], xp)

    def y_copy(s, i):
        return remote(block(i), block(i), y_sem.at[0, s], y_sem.at[1, s], yp)

    def fx_copy(s, i):
        return remote(bit(q_all, i, 1), bit(q_all, i, 1), fx_sem.at[0, s], fx_sem.at[1, s], xp)

    def fy_copy(s, i):
        return remote(bit(q_all, i, 0), bit(q_all, i, 0), fy_sem.at[0, s], fy_sem.at[1, s], yp)

    @pl.loop(1, na)
    def _(s):
        z_copy(s, me).start()

    x_copy(0, me).start()
    y_copy(0, me).start()

    q_square = jnp.sum(q_proj[...] * q_proj[...], axis=1, keepdims=True)
    square_rows = jnp.broadcast_to(q_square, (rows, tile))
    square_lanes = jnp.concatenate([square_rows] * group, axis=0).T
    lane = lax.broadcasted_iota(jnp.int32, (16, tile), 1)
    sub = lax.broadcasted_iota(jnp.int32, (16, tile), 0)
    own_list = jnp.where(sub == 10, square_lanes[0:16, :], lists_ref[...])
    slots[me] = jnp.where(lane // rows == b, own_list, 0.0)

    def list_copy(k, i):
        to = {"dp": lax.rem(me + k, n)}
        return remote(slots.at[i], slots.at[i], list_sem.at[0, k], list_sem.at[1, k], to)

    def before(k):
        return lax.rem(me - k + n, n)

    @pl.loop(1, n)
    def _(k):
        list_copy(k, me).start()

    p_load.wait()
    p_chunk = 256
    p_steps = width // p_chunk
    psq[...] = jnp.zeros_like(psq)
    for j in range(p_steps):
        at = slice(j * p_chunk, (j + 1) * p_chunk)
        out = dot(ps[...], w[:, at])
        p_proj[:, at] = out
        p_half[:, at] = out.astype(bf16)
        psq[...] += jnp.broadcast_to(jnp.sum(out * out, axis=1, keepdims=True), psq.shape)
        lo = 1 + j * (na - 1) // p_steps
        hi = 1 + (j + 1) * (na - 1) // p_steps

        @pl.loop(lo, hi)
        def _(s):
            z_copy(s, column(s)).wait_recv()
            x_copy(s, column(s)).start()
            y_copy(s, column(s)).start()

    psq_copy = remote(psq, psq_far, pair.at[0], pair.at[1], other)
    psq_copy.start()

    @pl.loop(0, na)
    def _(s):
        x_copy(s, column(s) + dx).wait_recv()
        fy_copy(s, column(s) + dx).start()
        y_copy(s, column(s) + dy).wait_recv()
        fx_copy(s, column(s) + dy).start()

    @pl.loop(1, n)
    def _(k):
        list_copy(k, before(k)).wait_recv()

    @pl.loop(0, na)
    def _(t):
        full = slots[t * group]
        for g in range(1, group):
            full = full + slots[t * group + g]
        lists[:, pl.ds(pl.multiple_of(t * tile, tile), tile)] = full

    def strip_of(i):
        return pl.ds(pl.multiple_of(i * strip, strip), strip)

    def numbers_of(i):
        first = me * p_rows + i * strip
        return (first + lax.broadcasted_iota(jnp.int32, (strip, 1), 0)).astype(f32)

    def is_own(i):
        return (lists[0:1, :] == numbers_of(i)).astype(f32)

    @pl.loop(0, p_rows // strip)
    def _(i):
        numbers = numbers_of(i)
        named = jnp.sum(is_own(i), axis=1, keepdims=True)
        col[strip_of(i), :] = jnp.broadcast_to(named, (strip, tile))
        times = (lists[1:2, :] == numbers).astype(f32)
        for k in range(2, names):
            times = times + (lists[k : k + 1, :] == numbers).astype(f32)
        g_q[strip_of(i), :] = times.astype(bf16)

    raw[p_rows : p_rows + 8, :] = jnp.broadcast_to(lists[10:11, :], (8, queries))
    psq_copy.wait_recv()

    @pl.loop(0, na)
    def _(s):
        fx_copy(s, column(s) + dx + dy).wait_recv()
        fy_copy(s, column(s) + dx + dy).wait_recv()

    s_chunk = 256

    @pl.loop(0, queries // s_chunk)
    def _(i):
        at = pl.ds(pl.multiple_of(i * s_chunk, s_chunk), s_chunk)
        raw[0:p_rows, at] = dot(p_half[...], q_all[at, :], by_rows)

    raw_copy = remote(raw, raw_far, pair.at[2], pair.at[3], other)
    raw_copy.start()
    raw_copy.wait()

    def q_scale():
        return lax.rsqrt(raw[p_rows : p_rows + 1, :] + raw_far[p_rows : p_rows + 1, :] + 1e-06)

    def p_scale(at):
        return lax.rsqrt(psq[at, 0:1] + psq_far[at, 0:1] + 1e-06)

    zero = jnp.zeros((1, queries), f32)

    def score_strip(i, sums):
        at = strip_of(i)
        scores = (raw[at, :] + raw_far[at, :]) * (q_scale() * (1.0 / temperature)) * p_scale(at)
        powers = (col[at, 0:1] + g_q[at, :].astype(f32)) * jnp.exp(scores)
        raw[at, :] = scores
        raw_far[at, :] = powers
        new = (powers, powers * scores, is_own(i) * scores)
        return tuple(s + jnp.sum(v, axis=0, keepdims=True) for s, v in zip(sums, new))

    total, moment, hit = lax.fori_loop(0, p_rows // strip, score_strip, (zero, zero, zero))

    t_slots[me] = total
    for t in range(na):
        at = slice(t * tile, (t + 1) * tile)
        mh[t] = jnp.concatenate([moment[:, at], hit[:, at], jnp.zeros((6, tile), f32)], axis=0)
    mh_slots[me] = mh[a]

    def t_copy(k, i):
        to = {"dp": lax.rem(me + k, n)}
        return remote(t_slots.at[i], t_slots.at[i], t_sem.at[0, k], t_sem.at[1, k], to)

    def mh_copy(k, i):
        peer = lax.rem(me + k, n)
        return remote(
            mh.at[peer // group], mh_slots.at[i], mh_sem.at[0, k], mh_sem.at[1, k], {"dp": peer}
        )

    @pl.loop(1, n)
    def _(k):
        t_copy(k, me).start()

    @pl.loop(1, n)
    def _(k):
        mh_copy(k, me).start()

    @pl.loop(1, n)
    def _(k):
        t_copy(k, before(k)).wait_recv()

    total = lax.fori_loop(0, n, lambda i, s: s + t_slots[i], zero)

    @pl.loop(0, p_rows // strip)
    def _(i):
        at = strip_of(i)
        slope = lists[9:10, :] * (1.0 / temperature)
        grads = slope * (raw_far[at, :] * (1.0 / total) - is_own(i))
        g_q[at, :] = (grads * p_scale(at)).astype(bf16)
        g_p[at, :] = (grads * q_scale()).astype(bf16)
        radial = temperature * jnp.sum(grads * raw[at, :], axis=1, keepdims=True)
        col[at, :] = jnp.broadcast_to(radial, (strip, tile))

    def owner(s):
        return lax.rem(a + s, na) * group + b

    def s1_copy(s, h, c):
        i = owner(s) + (dx if h else dy) + (dx + dy - (dx if h else dy)) * c
        return remote(
            bit(part, i, h),
            r1.at[s, h, c],
            s1_sem.at[0, s, 2 * h + c],
            s1_sem.at[1, s, 2 * h + c],
            xp if h else yp,
        )

    def s2_copy(s, h):
        i = owner(s) + (dy if h else dx)
        return remote(
            bit(part, i, h), r2.at[s, h], s2_sem.at[0, s, h], s2_sem.at[1, s, h], yp if h else xp
        )

    def s3_copy(s):
        i = owner(s)
        src = part.at[pl.ds(pl.multiple_of(i * rows, rows), rows), :]
        return remote(src, r3.at[s], s3_sem.at[0, s], s3_sem.at[1, s], {"dp": i})

    @pl.loop(0, na)
    def _(j):
        s = lax.rem(j + 1, na)
        at = pl.ds(pl.multiple_of(lax.rem(a + s, na) * tile, tile), tile)
        part[at, :] = dot(g_q[:, at], p_half[...], by_first).astype(bf16)
        for c in (1, 0):
            for h in range(2):
                s1_copy(s, h, c).start()

    for j in range(p_steps):
        at = slice(j * p_chunk, (j + 1) * p_chunk)
        grad = dot(g_p[...], q_all[:, at])
        inv = p_scale(slice(0, p_rows))
        p_dir[:, at] = (inv * (grad - p_proj[:, at] * (inv * col[:, 0:1]))).astype(bf16)

    @pl.loop(0, na)
    def _(j):
        s = lax.rem(j + 1, na)
        for h in range(2):
            s1_copy(s, h, 1).wait_recv()
            ref = bit(part, owner(s) + (dy if h else dx), h)
            ref[...] = (ref[...].astype(f32) + r1[s, h, 1].astype(f32)).astype(bf16)
            s2_copy(s, h).start()

    out_chunk = p_send.shape[2]
    out_steps = half // out_chunk

    def back_rows(which, c):
        return pl.ds(pl.multiple_of(which * half + c * out_chunk, out_chunk), out_chunk)

    def p_copy(c):
        return remote(p_send.at[c], p_recv.at[c], back_sem.at[0, c], back_sem.at[1, c], other)

    @pl.loop(0, out_steps)
    def _(c):
        p_send[c] = dot(p_dir[...], w[back_rows(1 - core, c), :], by_rows).astype(bf16)
        p_copy(c).start()

    def first_sum(s, h):
        s1_copy(s, h, 0).wait_recv()
        s2_copy(s, h).wait_recv()
        mine = bit(part, owner(s), h)[...].astype(f32)
        return mine + r1[s, h, 0].astype(f32) + r2[s, h].astype(f32)

    @pl.loop(1, na)
    def _(s):
        for h in range(2):
            bit(part, owner(s), h)[...] = first_sum(s, h).astype(bf16)
        s3_copy(s).start()

    for h in range(2):
        q_grad[h * piece : (h + 1) * piece, :] = first_sum(0, h)

    @pl.loop(0, out_steps)
    def _(c):
        kept = dot(p_dir[...], w[back_rows(core, c), :], by_rows)
        p_copy(c).wait_recv()
        at = pl.ds(pl.multiple_of(c * out_chunk, out_chunk), out_chunk)
        p_out[:, at] = (kept + p_recv[c].astype(f32)).astype(bf16)

    @pl.loop(1, n)
    def _(k):
        mh_copy(k, before(k)).wait_recv()

    sums = lax.fori_loop(0, n, lambda i, s: s + mh_slots[i], jnp.zeros((8, tile), f32))
    at = pl.ds(pl.multiple_of(a * tile, tile), tile)
    t_own = lax.fori_loop(
        0, n, lambda i, s: s + t_slots[i, :, at], jnp.zeros((1, tile), f32)
    )
    inv = lax.rsqrt(raw[p_rows : p_rows + 1, at] + raw_far[p_rows : p_rows + 1, at] + 1e-06)
    own_moment, own_hit = sums[0:1, :], sums[1:2, :]
    loss = jnp.log(t_own) - own_hit
    radial = lists[9:10, at] * (own_moment / t_own - own_hit)
    three = jnp.concatenate([loss, inv, inv * radial, jnp.zeros((5, tile), f32)], axis=0)
    turn[...] = jnp.concatenate([three] * (tile // 8), axis=0).T
    mine = turn[pl.ds(pl.multiple_of(b * rows, rows), rows), :]
    loss_ref[...] = mine

    @pl.loop(1, na)
    def _(s):
        s3_copy(s).wait_recv()
        q_grad[...] += r3[s].astype(f32)

    q_dir = (mine[:, 1:2] * (q_grad[...] - q_proj[...] * mine[:, 2:3])).astype(bf16)
    qs[:, 0:width] = q_dir

    q_copy = remote(q_send, q_recv, pair.at[4], pair.at[5], other)

    @pl.loop(0, out_steps)
    def _(c):
        to = pl.ds(pl.multiple_of(c * out_chunk, out_chunk), out_chunk)
        q_send[:, to] = dot(qs[:, 0:width], w[back_rows(1 - core, c), :], by_rows).astype(bf16)

    q_copy.start()

    @pl.loop(0, out_steps)
    def _(c):
        to = pl.ds(pl.multiple_of(c * out_chunk, out_chunk), out_chunk)
        q_grad[:, 0:out_chunk] = dot(qs[:, 0:width], w[back_rows(core, c), :], by_rows)
        q_out[:, to] = q_grad[:, 0:out_chunk].astype(bf16)

    q_copy.wait_recv()
    q_out[...] = (q_out[...].astype(f32) + q_recv[...].astype(f32)).astype(bf16)

    q_copy.wait_send()
    psq_copy.wait_send()

    @pl.loop(0, out_steps)
    def _(c):
        p_copy(c).wait_send()

    @pl.loop(1, n)
    def _(k):
        list_copy(k, me).wait_send()
        t_copy(k, me).wait_send()
        mh_copy(k, me).wait_send()

    @pl.loop(0, na)
    def _(s):
        x_copy(s, column(s)).wait_send()
        y_copy(s, column(s)).wait_send()
        fy_copy(s, column(s) + dx).wait_send()
        fx_copy(s, column(s) + dy).wait_send()
        for h in range(2):
            s1_copy(s, h, 0).wait_send()
            s1_copy(s, h, 1).wait_send()
            s2_copy(s, h).wait_send()

    @pl.loop(1, na)
    def _(s):
        z_copy(s, me).wait_send()
        s3_copy(s).wait_send()


def per_device(
    n, query_states, passage_states, head_weight, positives, negatives, search_cost_incoming_slope
):
    rows, depth = query_states.shape
    p_rows = passage_states.shape[0]
    width = head_weight.shape[1]
    half = depth // 2
    queries = n * rows
    group = tile // rows
    na = n // group
    piece = rows // 2
    names = 1 + negatives.shape[1]
    steps = 4
    lists = jnp.concatenate(
        [
            positives[None, :].astype(f32),
            negatives.T.astype(f32),
            search_cost_incoming_slope[None, :],
            jnp.zeros((16 - names - 1, rows), f32),
        ],
        axis=0,
    )
    lists = jnp.concatenate([lists] * group, axis=1)
    dma = pltpu.SemaphoreType.DMA
    vmem = pltpu.VMEM
    flops = 2 * width * (2 * (rows + p_rows) * depth + 3 * queries * p_rows)
    out = pl.pallas_call(
        functools.partial(kernel, n, names),
        out_shape=(
            jax.ShapeDtypeStruct((rows, tile), f32),
            jax.ShapeDtypeStruct((rows, half), bf16),
            jax.ShapeDtypeStruct((p_rows, half), bf16),
        ),
        in_specs=[pl.BlockSpec(memory_space=pl.ANY)] * 3
        + [pl.BlockSpec(memory_space=pltpu.VMEM)],
        out_specs=[pl.BlockSpec(memory_space=pltpu.VMEM)] * 3,
        scratch_shapes=[
            vmem((rows, depth), bf16),
            vmem((p_rows, depth), bf16),
            vmem((depth, width), bf16),
            vmem((rows, width), f32),
            vmem((queries, width), bf16),
            vmem((p_rows, width), f32),
            vmem((p_rows, width), bf16),
            vmem((p_rows, width), bf16),
            vmem((n, 16, tile), f32),
            vmem((16, queries), f32),
            vmem((p_rows, tile), f32),
            vmem((p_rows, tile), f32),
            vmem((p_rows, tile), f32),
            vmem((p_rows + 8, queries), f32),
            vmem((p_rows + 8, queries), f32),
            vmem((p_rows, queries), bf16),
            vmem((p_rows, queries), bf16),
            vmem((n, 1, queries), f32),
            vmem((na, 8, tile), f32),
            vmem((n, 8, tile), f32),
            vmem((tile, tile), f32),
            vmem((queries, width), bf16),
            vmem((na, 2, 2, piece, width), bf16),
            vmem((na, 2, piece, width), bf16),
            vmem((na, rows, width), bf16),
            vmem((rows, width), f32),
            vmem((steps, p_rows, half // steps), bf16),
            vmem((steps, p_rows, half // steps), bf16),
            vmem((rows, half), bf16),
            vmem((rows, half), bf16),
            dma((w_parts + 2,)),
            dma((6,)),
            dma((2, na)),
            dma((2, na)),
            dma((2, na)),
            dma((2, na)),
            dma((2, na)),
            dma((2, n)),
            dma((2, n)),
            dma((2, n)),
            dma((2, na, 4)),
            dma((2, na, 2)),
            dma((2, na)),
            dma((2, steps)),
        ],
        compiler_params=pltpu.CompilerParams(
            collective_id=0, has_side_effects=True, vmem_limit_bytes=60 * 2**20
        ),
        cost_estimate=pl.CostEstimate(
            flops=flops, bytes_accessed=12 * 2**20, transcendentals=queries * p_rows
        ),
        name="contrastive",
    )(query_states, passage_states, head_weight, lists)
    return out[0][:, 0], out[1], out[2]


def solution(mesh):
    placed = (P("dp", None), P("dp", None), P(None, "mp"), P("dp"), P("dp", None), P("dp"))
    return jax.shard_map(
        functools.partial(per_device, mesh.shape["dp"]),
        mesh=mesh,
        in_specs=placed,
        out_specs=(P("dp"), P("dp", "mp"), P("dp", "mp")),
        check_vma=False,
    )
```

```python
import functools

import jax
import jax.numpy as jnp
from jax import lax
from jax.experimental import pallas as pl
from jax.experimental.pallas import tpu as pltpu
from jax.sharding import PartitionSpec as P

temperature = 0.02
by_rows = (((1,), (1,)), ((), ()))
by_first = (((0,), (0,)), ((), ()))
f32 = jnp.float32
bf16 = jnp.bfloat16
tile = 128
w_parts = 8
window = 4
strip = 32
s_chunk = 512


def dot(x, y, dims=(((1,), (0,)), ((), ()))):
    return lax.dot_general(x, y, dims, preferred_element_type=f32)


def remote(src, dst, send, recv, where):
    return pltpu.make_async_remote_copy(
        src_ref=src,
        dst_ref=dst,
        send_sem=send,
        recv_sem=recv,
        device_id=where,
        device_id_type=pl.DeviceIdType.MESH,
    )


def kernel(
    n,
    names,
    q_hbm,
    p_hbm,
    w_hbm,
    pos_ref,
    neg_ref,
    slope_ref,
    loss_ref,
    q_out,
    p_out,
    qs,
    ps,
    w,
    q_proj,
    q_all,
    p_proj,
    p_half,
    p_dir,
    slots,
    sq_slots,
    lists,
    psq,
    psq_far,
    col,
    raw,
    raw_far,
    g_q,
    g_p,
    t_slots,
    mh,
    mh_slots,
    turn,
    part,
    r1,
    r2,
    r3,
    q_grad,
    p_send,
    p_recv,
    q_send,
    q_recv,
    p_done,
    load,
    pair,
    raw_sem,
    z_sem,
    x_sem,
    y_sem,
    fx_sem,
    fy_sem,
    list_sem,
    sq_sem,
    t_sem,
    mh_sem,
    s1_sem,
    s2_sem,
    s3_sem,
    back_sem,
    q_sem,
    done_sem,
):
    rows, depth = qs.shape
    p_rows, width = p_proj.shape
    queries = q_all.shape[0]
    piece = rows // 2
    group = tile // rows
    na = n // group
    half = depth // 2
    me = lax.axis_index("dp")
    core = lax.axis_index("mp")
    a, b = me // group, lax.rem(me, group)
    x, y = lax.rem(me, 2), lax.rem(me // 2, 2)
    dx, dy = 1 - 2 * x, 2 - 4 * y
    xp, yp, other = {"dp": me + dx}, {"dp": me + dy}, {"mp": 1 - core}

    k_rows = depth // w_parts

    def w_load(i):
        at = pl.ds(pl.multiple_of(i * k_rows, k_rows), k_rows)
        return pltpu.make_async_copy(w_hbm.at[at, :], w.at[at, :], load.at[i])

    q_load = pltpu.make_async_copy(q_hbm, qs, load.at[w_parts])
    p_load = pltpu.make_async_copy(p_hbm, ps, load.at[w_parts + 1])
    q_load.start()
    for i in range(window):
        w_load(i).start()

    barrier = pltpu.get_barrier_semaphore()

    @pl.loop(1, n)
    def _(k):
        pl.semaphore_signal(
            barrier,
            inc=1,
            device_id={"dp": lax.rem(me + k, n)},
            device_id_type=pl.DeviceIdType.MESH,
        )

    pl.semaphore_signal(
        barrier, inc=1, device_id=other, device_id_type=pl.DeviceIdType.MESH
    )

    def before(k):
        return lax.rem(me - k + n, n)

    def list_copy(k, i):
        to = {"dp": lax.rem(me + k, n)}
        return remote(slots.at[i], slots.at[i], list_sem.at[0, k], list_sem.at[1, k], to)

    def sq_copy(k, i):
        to = {"dp": lax.rem(me + k, n)}
        return remote(sq_slots.at[i], sq_slots.at[i], sq_sem.at[0, k], sq_sem.at[1, k], to)

    turn[0:24, :] = jnp.zeros((24, tile), f32)
    turn[0 : names - 1, 0:rows] = neg_ref[...].astype(f32)
    turn[8:9, 0:rows] = pos_ref[...].astype(f32)
    turn[16:17, 0:rows] = slope_ref[...]
    neg_lanes, pos_lanes, slope_lanes = [
        pltpu.roll(turn[8 * i : 8 * i + 8, :], b * rows, 1) for i in range(3)
    ]
    lane = lax.broadcasted_iota(jnp.int32, (1, tile), 1)
    mask = lane // rows == b
    slots[me] = jnp.concatenate(
        [
            pos_lanes[0:1, :],
            neg_lanes[0 : names - 1, :],
            slope_lanes[0:1, :],
            jnp.zeros((15 - names, tile), f32),
        ],
        axis=0,
    )
    pl.semaphore_wait(barrier, n)

    @pl.loop(1, n)
    def _(k):
        list_copy(k, me).start()

    q_load.wait()
    q_proj[...] = jnp.zeros_like(q_proj)

    @pl.loop(0, w_parts)
    def _(i):
        w_load(i).wait()

        @pl.when(i < w_parts - window)
        def _():
            w_load(i + window).start()

        @pl.when(i == w_parts - window)
        def _():
            p_load.start()

        at = pl.ds(pl.multiple_of(i * k_rows, k_rows), k_rows)
        q_proj[...] += dot(qs[:, at], w[at, :])

    def block(i):
        return q_all.at[pl.ds(pl.multiple_of(i * rows, rows), rows), :]

    def bit(ref, i, h):
        return ref.at[pl.ds(pl.multiple_of(i * rows + h * piece, piece), piece), :]

    q_all[pl.ds(pl.multiple_of(me * rows, rows), rows), :] = q_proj[...].astype(bf16)
    def z_copy(s, i):
        to = {"dp": lax.rem(a + s, na) * group + b}
        return remote(block(i), block(i), z_sem.at[0, s], z_sem.at[1, s], to)

    def column(s):
        return lax.rem(a - s + na, na) * group + b

    def x_copy(s, i):
        return remote(block(i), block(i), x_sem.at[0, s], x_sem.at[1, s], xp)

    def y_copy(s, i):
        return remote(block(i), block(i), y_sem.at[0, s], y_sem.at[1, s], yp)

    def fx_copy(s, i):
        return remote(bit(q_all, i, 1), bit(q_all, i, 1), fx_sem.at[0, s], fx_sem.at[1, s], xp)

    def fy_copy(s, i):
        return remote(bit(q_all, i, 0), bit(q_all, i, 0), fy_sem.at[0, s], fy_sem.at[1, s], yp)

    @pl.loop(1, na)
    def _(s):
        z_copy(s, me).start()

    x_copy(0, me).start()
    y_copy(0, me).start()

    q_square = jnp.sum(q_proj[...] * q_proj[...], axis=1, keepdims=True)
    square_rows = jnp.broadcast_to(q_square, (rows, tile))
    square_lanes = jnp.concatenate([square_rows] * group, axis=0).T
    sq_slots[me] = jnp.where(mask, square_lanes[0:1, :], 0.0)

    @pl.loop(1, n)
    def _(k):
        sq_copy(k, me).start()

    p_load.wait()
    p_chunk = 256
    p_steps = width // p_chunk
    psq[...] = jnp.zeros_like(psq)
    for j in range(p_steps):
        at = slice(j * p_chunk, (j + 1) * p_chunk)
        out = dot(ps[...], w[:, at])
        p_proj[:, at] = out
        p_half[:, at] = out.astype(bf16)
        psq[...] += jnp.broadcast_to(jnp.sum(out * out, axis=1, keepdims=True), psq.shape)
        lo = 1 + j * (na - 1) // p_steps
        hi = 1 + (j + 1) * (na - 1) // p_steps

        @pl.loop(lo, hi)
        def _(s):
            z_copy(s, column(s)).wait_recv()
            x_copy(s, column(s)).start()
            y_copy(s, column(s)).start()

    psq_copy = remote(psq, psq_far, pair.at[0], pair.at[1], other)
    psq_copy.start()

    @pl.loop(0, na)
    def _(s):
        x_copy(s, column(s) + dx).wait_recv()
        fy_copy(s, column(s) + dx).start()
        y_copy(s, column(s) + dy).wait_recv()
        fx_copy(s, column(s) + dy).start()

    @pl.loop(1, n)
    def _(k):
        list_copy(k, before(k)).wait_recv()
        sq_copy(k, before(k)).wait_recv()

    @pl.loop(0, na)
    def _(t):
        at = pl.ds(pl.multiple_of(t * tile, tile), tile)
        full, square = slots[t * group], sq_slots[t * group]
        for g in range(1, group):
            full = full + slots[t * group + g]
            square = square + sq_slots[t * group + g]
        lists[:, at] = full
        raw[p_rows : p_rows + 8, at] = jnp.broadcast_to(square, (8, tile))

    def strip_of(i):
        return pl.ds(pl.multiple_of(i * strip, strip), strip)

    def numbers_of(i):
        first = me * p_rows + i * strip
        return (first + lax.broadcasted_iota(jnp.int32, (strip, 1), 0)).astype(f32)

    def is_own(i):
        return (lists[0:1, :] == numbers_of(i)).astype(f32)

    @pl.loop(0, p_rows // strip)
    def _(i):
        numbers = numbers_of(i)
        named = jnp.sum(is_own(i), axis=1, keepdims=True)
        col[strip_of(i), :] = jnp.broadcast_to(named, (strip, tile))
        times = (lists[1:2, :] == numbers).astype(f32)
        for k in range(2, names):
            times = times + (lists[k : k + 1, :] == numbers).astype(f32)
        g_q[strip_of(i), :] = times.astype(bf16)

    psq_copy.wait_recv()

    @pl.loop(0, na)
    def _(s):
        fx_copy(s, column(s) + dx + dy).wait_recv()
        fy_copy(s, column(s) + dx + dy).wait_recv()

    s_rows = p_rows // 2
    sq_far_copy = remote(
        raw.at[p_rows : p_rows + 8, :], raw_far.at[p_rows : p_rows + 8, :], pair.at[4], pair.at[5], other
    )
    sq_far_copy.start()

    def raw_copy(i):
        at = pl.ds(pl.multiple_of(i * s_rows, s_rows), s_rows)
        return remote(raw.at[at, :], raw_far.at[at, :], raw_sem.at[0, i], raw_sem.at[1, i], other)

    for i in range(2):
        at = slice(i * s_rows, (i + 1) * s_rows)
        for j in range(queries // s_chunk):
            to = slice(j * s_chunk, (j + 1) * s_chunk)
            raw[at, to] = dot(p_half[at, :], q_all[to, :], by_rows)
        raw_copy(i).start()

    sq_far_copy.wait()

    def q_scale():
        return lax.rsqrt(raw[p_rows : p_rows + 1, :] + raw_far[p_rows : p_rows + 1, :] + 1e-06)

    def p_scale(at):
        return lax.rsqrt(psq[at, 0:1] + psq_far[at, 0:1] + 1e-06)

    zero = jnp.zeros((1, queries), f32)

    def score_strip(i, sums):
        at = strip_of(i)
        scores = (raw[at, :] + raw_far[at, :]) * (q_scale() * (1.0 / temperature)) * p_scale(at)
        powers = (col[at, 0:1] + g_q[at, :].astype(f32)) * jnp.exp(scores)
        raw[at, :] = scores
        raw_far[at, :] = powers
        new = (powers, powers * scores, is_own(i) * scores)
        return tuple(s + jnp.sum(v, axis=0, keepdims=True) for s, v in zip(sums, new))

    sums = (zero, zero, zero)
    s_strips = s_rows // strip
    for i in range(2):
        raw_copy(i).wait()
        sums = lax.fori_loop(i * s_strips, (i + 1) * s_strips, score_strip, sums)
    total, moment, hit = sums

    t_slots[me] = total
    for t in range(na):
        at = slice(t * tile, (t + 1) * tile)
        mh[t] = jnp.concatenate([moment[:, at], hit[:, at], jnp.zeros((6, tile), f32)], axis=0)
    mh_slots[me] = mh[a]

    def t_copy(k, i):
        to = {"dp": lax.rem(me + k, n)}
        return remote(t_slots.at[i], t_slots.at[i], t_sem.at[0, k], t_sem.at[1, k], to)

    def mh_copy(k, i):
        peer = lax.rem(me + k, n)
        return remote(
            mh.at[peer // group], mh_slots.at[i], mh_sem.at[0, k], mh_sem.at[1, k], {"dp": peer}
        )

    @pl.loop(1, n)
    def _(k):
        t_copy(k, me).start()

    @pl.loop(1, n)
    def _(k):
        mh_copy(k, me).start()

    @pl.loop(1, n)
    def _(k):
        t_copy(k, before(k)).wait_recv()

    total = lax.fori_loop(0, n, lambda i, s: s + t_slots[i], zero)

    @pl.loop(0, p_rows // strip)
    def _(i):
        at = strip_of(i)
        slope = lists[9:10, :] * (1.0 / temperature)
        grads = slope * (raw_far[at, :] * (1.0 / total) - is_own(i))
        g_q[at, :] = (grads * p_scale(at)).astype(bf16)
        g_p[at, :] = (grads * q_scale()).astype(bf16)
        radial = temperature * jnp.sum(grads * raw[at, :], axis=1, keepdims=True)
        col[at, :] = jnp.broadcast_to(radial, (strip, tile))

    def owner(s):
        return lax.rem(a + s, na) * group + b

    def s1_copy(s, h, c):
        i = owner(s) + (dx if h else dy) + (dx + dy - (dx if h else dy)) * c
        return remote(
            bit(part, i, h),
            r1.at[s, h, c],
            s1_sem.at[0, s, 2 * h + c],
            s1_sem.at[1, s, 2 * h + c],
            xp if h else yp,
        )

    def s2_copy(s, h):
        i = owner(s) + (dy if h else dx)
        return remote(
            bit(part, i, h), r2.at[s, h], s2_sem.at[0, s, h], s2_sem.at[1, s, h], yp if h else xp
        )

    def s3_copy(s):
        i = owner(s)
        src = part.at[pl.ds(pl.multiple_of(i * rows, rows), rows), :]
        return remote(src, r3.at[s], s3_sem.at[0, s], s3_sem.at[1, s], {"dp": i})

    @pl.loop(0, na)
    def _(j):
        s = lax.rem(j + 1, na)
        at = pl.ds(pl.multiple_of(lax.rem(a + s, na) * tile, tile), tile)
        part[at, :] = dot(g_q[:, at], p_half[...], by_first).astype(bf16)
        for c in (1, 0):
            for h in range(2):
                s1_copy(s, h, c).start()

    for j in range(p_steps):
        at = slice(j * p_chunk, (j + 1) * p_chunk)
        grad = dot(g_p[...], q_all[:, at])
        inv = p_scale(slice(0, p_rows))
        p_dir[:, at] = (inv * (grad - p_proj[:, at] * (inv * col[:, 0:1]))).astype(bf16)

    out_chunk = p_send.shape[2]
    out_steps = half // out_chunk

    def back_rows(which, c):
        return pl.ds(pl.multiple_of(which * half + c * out_chunk, out_chunk), out_chunk)

    def p_copy(c):
        return remote(p_send.at[c], p_recv.at[c], back_sem.at[0, c], back_sem.at[1, c], other)

    def p_far(c):
        p_send[c] = dot(p_dir[...], w[back_rows(1 - core, c), :], by_rows).astype(bf16)
        p_copy(c).start()

    def first_sum(s, h):
        s1_copy(s, h, 0).wait_recv()
        s2_copy(s, h).wait_recv()
        mine = bit(part, owner(s), h)[...].astype(f32)
        return mine + r1[s, h, 0].astype(f32) + r2[s, h].astype(f32)

    @pl.loop(0, na)
    def _(j):
        s = lax.rem(j + 1, na)
        for h in range(2):
            s1_copy(s, h, 1).wait_recv()
            ref = bit(part, owner(s) + (dy if h else dx), h)
            ref[...] = (ref[...].astype(f32) + r1[s, h, 1].astype(f32)).astype(bf16)
            s2_copy(s, h).start()

        @pl.when(j < out_steps)
        def _():
            p_far(j)

        @pl.when(j >= 1)
        def _():
            for h in range(2):
                bit(part, owner(j), h)[...] = first_sum(j, h).astype(bf16)
            s3_copy(j).start()

    for c in range(na, out_steps):
        p_far(c)

    for h in range(2):
        q_grad[h * piece : (h + 1) * piece, :] = first_sum(0, h)

    def done_copy(c):
        at = pl.ds(pl.multiple_of(c * out_chunk, out_chunk), out_chunk)
        return pltpu.make_async_copy(p_done.at[c], p_out.at[:, at], done_sem.at[c])

    @pl.loop(0, out_steps)
    def _(c):
        kept = dot(p_dir[...], w[back_rows(core, c), :], by_rows)
        p_copy(c).wait_recv()
        p_done[c] = (kept + p_recv[c].astype(f32)).astype(bf16)
        done_copy(c).start()

    @pl.loop(1, n)
    def _(k):
        mh_copy(k, before(k)).wait_recv()

    sums = lax.fori_loop(0, n, lambda i, s: s + mh_slots[i], jnp.zeros((8, tile), f32))
    at = pl.ds(pl.multiple_of(a * tile, tile), tile)
    t_own = lax.fori_loop(
        0, n, lambda i, s: s + t_slots[i, :, at], jnp.zeros((1, tile), f32)
    )
    inv = lax.rsqrt(raw[p_rows : p_rows + 1, at] + raw_far[p_rows : p_rows + 1, at] + 1e-06)
    own_moment, own_hit = sums[0:1, :], sums[1:2, :]
    loss = jnp.log(t_own) - own_hit
    radial = lists[9:10, at] * (own_moment / t_own - own_hit)
    three = jnp.concatenate([loss, inv, inv * radial, jnp.zeros((5, tile), f32)], axis=0)
    turn[...] = jnp.concatenate([three] * (tile // 8), axis=0).T
    mine = turn[pl.ds(pl.multiple_of(b * rows, rows), rows), :]
    loss_ref[...] = pltpu.roll(three, lax.rem(tile - b * rows, tile), 1)[0:1, 0:rows]

    @pl.loop(1, na)
    def _(s):
        s3_copy(s).wait_recv()
        q_grad[...] += r3[s].astype(f32)

    q_dir = (mine[:, 1:2] * (q_grad[...] - q_proj[...] * mine[:, 2:3])).astype(bf16)
    qs[:, 0:width] = q_dir

    def q_copy(c):
        return remote(q_send.at[c], q_recv.at[c], q_sem.at[0, c], q_sem.at[1, c], other)

    @pl.loop(0, out_steps)
    def _(c):
        q_send[c] = dot(qs[:, 0:width], w[back_rows(1 - core, c), :], by_rows).astype(bf16)
        q_copy(c).start()

    @pl.loop(0, out_steps)
    def _(c):
        to = pl.ds(pl.multiple_of(c * out_chunk, out_chunk), out_chunk)
        kept = dot(qs[:, 0:width], w[back_rows(core, c), :], by_rows)
        q_copy(c).wait_recv()
        q_out[:, to] = (kept + q_recv[c].astype(f32)).astype(bf16)

    psq_copy.wait_send()

    @pl.loop(0, out_steps)
    def _(c):
        p_copy(c).wait_send()
        q_copy(c).wait_send()
        done_copy(c).wait()

    @pl.loop(1, n)
    def _(k):
        list_copy(k, me).wait_send()
        sq_copy(k, me).wait_send()
        t_copy(k, me).wait_send()
        mh_copy(k, me).wait_send()

    @pl.loop(0, na)
    def _(s):
        x_copy(s, column(s)).wait_send()
        y_copy(s, column(s)).wait_send()
        fy_copy(s, column(s) + dx).wait_send()
        fx_copy(s, column(s) + dy).wait_send()
        for h in range(2):
            s1_copy(s, h, 0).wait_send()
            s1_copy(s, h, 1).wait_send()
            s2_copy(s, h).wait_send()

    @pl.loop(1, na)
    def _(s):
        z_copy(s, me).wait_send()
        s3_copy(s).wait_send()


def hand_over(loss, q, p, loss_out, q_out, p_out, sems):
    parts = sems.shape[0] - 2
    size = p.shape[0] // parts
    copies = [
        pltpu.make_async_copy(loss, loss_out, sems.at[0]),
        pltpu.make_async_copy(q, q_out, sems.at[1]),
    ]
    for i in range(parts):
        at = slice(i * size, (i + 1) * size)
        copies.append(pltpu.make_async_copy(p.at[at, :], p_out.at[at, :], sems.at[2 + i]))
    for copy in copies:
        copy.start()
    for copy in copies:
        copy.wait()


def per_device(
    n, query_states, passage_states, head_weight, positives, negatives, search_cost_incoming_slope
):
    rows, depth = query_states.shape
    p_rows = passage_states.shape[0]
    width = head_weight.shape[1]
    half = depth // 2
    queries = n * rows
    group = tile // rows
    na = n // group
    piece = rows // 2
    names = 1 + negatives.shape[1]
    steps = 4
    dma = pltpu.SemaphoreType.DMA
    vmem = pltpu.VMEM
    flops = 2 * width * (2 * (rows + p_rows) * depth + 3 * queries * p_rows)
    out = pl.pallas_call(
        functools.partial(kernel, n, names),
        out_shape=(
            jax.ShapeDtypeStruct((1, rows), f32),
            jax.ShapeDtypeStruct((rows, half), bf16),
            jax.ShapeDtypeStruct((p_rows, half), bf16),
        ),
        in_specs=[pl.BlockSpec(memory_space=pl.ANY)] * 3
        + [pl.BlockSpec(memory_space=pltpu.VMEM)] * 3,
        out_specs=[pl.BlockSpec(memory_space=pltpu.VMEM)] * 2
        + [pl.BlockSpec(memory_space=pl.ANY)],
        scratch_shapes=[
            vmem((rows, depth), bf16),
            vmem((p_rows, depth), bf16),
            vmem((depth, width), bf16),
            vmem((rows, width), f32),
            vmem((queries, width), bf16),
            vmem((p_rows, width), f32),
            vmem((p_rows, width), bf16),
            vmem((p_rows, width), bf16),
            vmem((n, 16, tile), f32),
            vmem((n, 1, tile), f32),
            vmem((16, queries), f32),
            vmem((p_rows, tile), f32),
            vmem((p_rows, tile), f32),
            vmem((p_rows, tile), f32),
            vmem((p_rows + 8, queries), f32),
            vmem((p_rows + 8, queries), f32),
            vmem((p_rows, queries), bf16),
            vmem((p_rows, queries), bf16),
            vmem((n, 1, queries), f32),
            vmem((na, 8, tile), f32),
            vmem((n, 8, tile), f32),
            vmem((tile, tile), f32),
            vmem((queries, width), bf16),
            vmem((na, 2, 2, piece, width), bf16),
            vmem((na, 2, piece, width), bf16),
            vmem((na, rows, width), bf16),
            vmem((rows, width), f32),
            vmem((steps, p_rows, half // steps), bf16),
            vmem((steps, p_rows, half // steps), bf16),
            vmem((steps, rows, half // steps), bf16),
            vmem((steps, rows, half // steps), bf16),
            vmem((steps, p_rows, half // steps), bf16),
            dma((w_parts + 2,)),
            dma((6,)),
            dma((2, 2)),
            dma((2, na)),
            dma((2, na)),
            dma((2, na)),
            dma((2, na)),
            dma((2, na)),
            dma((2, n)),
            dma((2, n)),
            dma((2, n)),
            dma((2, n)),
            dma((2, na, 4)),
            dma((2, na, 2)),
            dma((2, na)),
            dma((2, steps)),
            dma((2, steps)),
            dma((steps,)),
        ],
        compiler_params=pltpu.CompilerParams(
            collective_id=0, has_side_effects=True, vmem_limit_bytes=60 * 2**20
        ),
        cost_estimate=pl.CostEstimate(
            flops=flops, bytes_accessed=12 * 2**20, transcendentals=queries * p_rows
        ),
        name="contrastive",
    )(
        query_states,
        passage_states,
        head_weight,
        positives.reshape(1, rows),
        negatives.T,
        search_cost_incoming_slope.reshape(1, rows),
    )
    losses, q_rows, p_rows_out = pl.pallas_call(
        hand_over,
        out_shape=tuple(jax.ShapeDtypeStruct(x.shape, x.dtype) for x in out),
        in_specs=[pl.BlockSpec(memory_space=pl.ANY)] * 3,
        out_specs=[pl.BlockSpec(memory_space=pl.ANY)] * 3,
        scratch_shapes=[dma((2 + steps,))],
        compiler_params=pltpu.CompilerParams(vmem_limit_bytes=60 * 2**20),
        name="hand_over",
    )(*out)
    return losses.reshape(rows), q_rows, p_rows_out


def solution(mesh):
    placed = (P("dp", None), P("dp", None), P(None, "mp"), P("dp"), P("dp", None), P("dp"))
    return jax.shard_map(
        functools.partial(per_device, mesh.shape["dp"]),
        mesh=mesh,
        in_specs=placed,
        out_specs=(P("dp"), P("dp", "mp"), P("dp", "mp")),
        check_vma=False,
    )
```

```python
import functools

import jax
import jax.numpy as jnp
from jax import lax
from jax.experimental import pallas as pl
from jax.experimental.pallas import tpu as pltpu
from jax.sharding import PartitionSpec as P

temperature = 0.02
by_rows = (((1,), (1,)), ((), ()))
by_first = (((0,), (0,)), ((), ()))
f32 = jnp.float32
bf16 = jnp.bfloat16
tile = 128
w_parts = 8
window = 4
strip = 32
s_chunk = 512


def dot(x, y, dims=(((1,), (0,)), ((), ()))):
    return lax.dot_general(x, y, dims, preferred_element_type=f32)


def remote(src, dst, send, recv, where):
    return pltpu.make_async_remote_copy(
        src_ref=src,
        dst_ref=dst,
        send_sem=send,
        recv_sem=recv,
        device_id=where,
        device_id_type=pl.DeviceIdType.MESH,
    )


def kernel(
    n,
    names,
    q_hbm,
    p_hbm,
    w_hbm,
    pos_ref,
    neg_ref,
    slope_ref,
    loss_ref,
    q_out,
    p_out,
    qs,
    ps,
    w,
    q_proj,
    q_all,
    p_proj,
    p_half,
    p_dir,
    slots,
    sq_slots,
    lists,
    psq,
    psq_far,
    col,
    raw,
    raw_far,
    g_q,
    g_p,
    t_slots,
    mh,
    mh_slots,
    turn,
    part,
    r1,
    r2,
    r3,
    q_grad,
    p_send,
    p_recv,
    q_send,
    q_recv,
    p_done,
    load,
    pair,
    raw_sem,
    z_sem,
    x_sem,
    y_sem,
    fx_sem,
    fy_sem,
    list_sem,
    sq_sem,
    t_sem,
    mh_sem,
    s1_sem,
    s2_sem,
    s3_sem,
    back_sem,
    q_sem,
    done_sem,
):
    rows, depth = qs.shape
    p_rows, width = p_proj.shape
    queries = q_all.shape[0]
    piece = rows // 2
    group = tile // rows
    na = n // group
    half = depth // 2
    me = lax.axis_index("dp")
    core = lax.axis_index("mp")
    a, b = me // group, lax.rem(me, group)
    x, y = lax.rem(me, 2), lax.rem(me // 2, 2)
    dx, dy = 1 - 2 * x, 2 - 4 * y
    xp, yp, other = {"dp": me + dx}, {"dp": me + dy}, {"mp": 1 - core}

    k_rows = depth // w_parts

    def w_load(i):
        at = pl.ds(pl.multiple_of(i * k_rows, k_rows), k_rows)
        return pltpu.make_async_copy(w_hbm.at[at, :], w.at[at, :], load.at[i])

    q_load = pltpu.make_async_copy(q_hbm, qs, load.at[w_parts])
    p_load = pltpu.make_async_copy(p_hbm, ps, load.at[w_parts + 1])
    q_load.start()
    for i in range(window):
        w_load(i).start()

    barrier = pltpu.get_barrier_semaphore()

    @pl.loop(1, n)
    def _(k):
        pl.semaphore_signal(
            barrier,
            inc=1,
            device_id={"dp": lax.rem(me + k, n)},
            device_id_type=pl.DeviceIdType.MESH,
        )

    pl.semaphore_signal(
        barrier, inc=1, device_id=other, device_id_type=pl.DeviceIdType.MESH
    )

    def before(k):
        return lax.rem(me - k + n, n)

    def list_copy(k, i):
        to = {"dp": lax.rem(me + k, n)}
        return remote(slots.at[i], slots.at[i], list_sem.at[0, k], list_sem.at[1, k], to)

    def sq_copy(k, i):
        to = {"dp": lax.rem(me + k, n)}
        return remote(sq_slots.at[i], sq_slots.at[i], sq_sem.at[0, k], sq_sem.at[1, k], to)

    turn[0:24, :] = jnp.zeros((24, tile), f32)
    turn[0 : names - 1, 0:rows] = neg_ref[...].astype(f32)
    turn[8:9, 0:rows] = pos_ref[...].astype(f32)
    turn[16:17, 0:rows] = slope_ref[...]
    neg_lanes, pos_lanes, slope_lanes = [
        pltpu.roll(turn[8 * i : 8 * i + 8, :], b * rows, 1) for i in range(3)
    ]
    lane = lax.broadcasted_iota(jnp.int32, (1, tile), 1)
    mask = lane // rows == b
    slots[me] = jnp.concatenate(
        [
            pos_lanes[0:1, :],
            neg_lanes[0 : names - 1, :],
            slope_lanes[0:1, :],
            jnp.zeros((15 - names, tile), f32),
        ],
        axis=0,
    )
    pl.semaphore_wait(barrier, n)

    @pl.loop(1, n)
    def _(k):
        list_copy(k, me).start()

    q_load.wait()
    q_proj[...] = jnp.zeros_like(q_proj)

    @pl.loop(0, w_parts)
    def _(i):
        w_load(i).wait()

        @pl.when(i < w_parts - window)
        def _():
            w_load(i + window).start()

        @pl.when(i == w_parts - window)
        def _():
            p_load.start()

        at = pl.ds(pl.multiple_of(i * k_rows, k_rows), k_rows)
        q_proj[...] += dot(qs[:, at], w[at, :])

    def block(i):
        return q_all.at[pl.ds(pl.multiple_of(i * rows, rows), rows), :]

    def bit(ref, i, h):
        return ref.at[pl.ds(pl.multiple_of(i * rows + h * piece, piece), piece), :]

    q_all[pl.ds(pl.multiple_of(me * rows, rows), rows), :] = q_proj[...].astype(bf16)
    def z_copy(s, i):
        to = {"dp": lax.rem(a + s, na) * group + b}
        return remote(block(i), block(i), z_sem.at[0, s], z_sem.at[1, s], to)

    def column(s):
        return lax.rem(a - s + na, na) * group + b

    def x_copy(s, i):
        return remote(block(i), block(i), x_sem.at[0, s], x_sem.at[1, s], xp)

    def y_copy(s, i):
        return remote(block(i), block(i), y_sem.at[0, s], y_sem.at[1, s], yp)

    def fx_copy(s, i):
        return remote(bit(q_all, i, 1), bit(q_all, i, 1), fx_sem.at[0, s], fx_sem.at[1, s], xp)

    def fy_copy(s, i):
        return remote(bit(q_all, i, 0), bit(q_all, i, 0), fy_sem.at[0, s], fy_sem.at[1, s], yp)

    @pl.loop(1, na)
    def _(s):
        z_copy(s, me).start()

    x_copy(0, me).start()
    y_copy(0, me).start()

    q_square = jnp.sum(q_proj[...] * q_proj[...], axis=1, keepdims=True)
    square_rows = jnp.broadcast_to(q_square, (rows, tile))
    square_lanes = jnp.concatenate([square_rows] * group, axis=0).T
    sq_slots[me] = jnp.where(mask, square_lanes[0:1, :], 0.0)

    @pl.loop(1, n)
    def _(k):
        sq_copy(k, me).start()

    p_load.wait()
    p_chunk = 256
    p_steps = width // p_chunk
    psq[...] = jnp.zeros_like(psq)
    for j in range(p_steps):
        at = slice(j * p_chunk, (j + 1) * p_chunk)
        out = dot(ps[...], w[:, at])
        p_proj[:, at] = out
        p_half[:, at] = out.astype(bf16)
        psq[...] += jnp.broadcast_to(jnp.sum(out * out, axis=1, keepdims=True), psq.shape)
        lo = 1 + j * (na - 1) // p_steps
        hi = 1 + (j + 1) * (na - 1) // p_steps

        @pl.loop(lo, hi)
        def _(s):
            z_copy(s, column(s)).wait_recv()
            x_copy(s, column(s)).start()
            y_copy(s, column(s)).start()

    psq_copy = remote(psq, psq_far, pair.at[0], pair.at[1], other)
    psq_copy.start()

    @pl.loop(0, na)
    def _(s):
        x_copy(s, column(s) + dx).wait_recv()
        fy_copy(s, column(s) + dx).start()
        y_copy(s, column(s) + dy).wait_recv()
        fx_copy(s, column(s) + dy).start()

    @pl.loop(1, n)
    def _(k):
        list_copy(k, before(k)).wait_recv()
        sq_copy(k, before(k)).wait_recv()

    @pl.loop(0, na)
    def _(t):
        at = pl.ds(pl.multiple_of(t * tile, tile), tile)
        full, square = slots[t * group], sq_slots[t * group]
        for g in range(1, group):
            full = full + slots[t * group + g]
            square = square + sq_slots[t * group + g]
        lists[:, at] = full
        raw[p_rows : p_rows + 8, at] = jnp.broadcast_to(square, (8, tile))

    def strip_of(i):
        return pl.ds(pl.multiple_of(i * strip, strip), strip)

    def numbers_of(i):
        first = me * p_rows + i * strip
        return (first + lax.broadcasted_iota(jnp.int32, (strip, 1), 0)).astype(f32)

    def is_own(i):
        return (lists[0:1, :] == numbers_of(i)).astype(f32)

    @pl.loop(0, p_rows // strip)
    def _(i):
        numbers = numbers_of(i)
        named = jnp.sum(is_own(i), axis=1, keepdims=True)
        col[strip_of(i), :] = jnp.broadcast_to(named, (strip, tile))
        times = (lists[1:2, :] == numbers).astype(f32)
        for k in range(2, names):
            times = times + (lists[k : k + 1, :] == numbers).astype(f32)
        g_q[strip_of(i), :] = times.astype(bf16)

    psq_copy.wait_recv()

    @pl.loop(0, na)
    def _(s):
        fx_copy(s, column(s) + dx + dy).wait_recv()
        fy_copy(s, column(s) + dx + dy).wait_recv()

    s_rows = p_rows // 2
    sq_far_copy = remote(
        raw.at[p_rows : p_rows + 8, :], raw_far.at[p_rows : p_rows + 8, :], pair.at[4], pair.at[5], other
    )
    sq_far_copy.start()

    def raw_copy(i):
        at = pl.ds(pl.multiple_of(i * s_rows, s_rows), s_rows)
        return remote(raw.at[at, :], raw_far.at[at, :], raw_sem.at[0, i], raw_sem.at[1, i], other)

    for i in range(2):
        at = slice(i * s_rows, (i + 1) * s_rows)
        for j in range(queries // s_chunk):
            to = slice(j * s_chunk, (j + 1) * s_chunk)
            raw[at, to] = dot(p_half[at, :], q_all[to, :], by_rows)
        raw_copy(i).start()

    sq_far_copy.wait()

    def q_scale():
        return lax.rsqrt(raw[p_rows : p_rows + 1, :] + raw_far[p_rows : p_rows + 1, :] + 1e-06)

    def p_scale(at):
        return lax.rsqrt(psq[at, 0:1] + psq_far[at, 0:1] + 1e-06)

    zero = jnp.zeros((1, queries), f32)

    def score_strip(i, sums):
        at = strip_of(i)
        scores = (raw[at, :] + raw_far[at, :]) * (q_scale() * (1.0 / temperature)) * p_scale(at)
        powers = (col[at, 0:1] + g_q[at, :].astype(f32)) * jnp.exp(scores)
        raw[at, :] = scores
        raw_far[at, :] = powers
        new = (powers, powers * scores, is_own(i) * scores)
        return tuple(s + jnp.sum(v, axis=0, keepdims=True) for s, v in zip(sums, new))

    sums = (zero, zero, zero)
    s_strips = s_rows // strip
    for i in range(2):
        raw_copy(i).wait()
        sums = lax.fori_loop(i * s_strips, (i + 1) * s_strips, score_strip, sums)
    total, moment, hit = sums

    t_slots[me] = total
    for t in range(na):
        at = slice(t * tile, (t + 1) * tile)
        mh[t] = jnp.concatenate([moment[:, at], hit[:, at], jnp.zeros((6, tile), f32)], axis=0)
    mh_slots[me] = mh[a]

    def t_copy(k, i):
        to = {"dp": lax.rem(me + k, n)}
        return remote(t_slots.at[i], t_slots.at[i], t_sem.at[0, k], t_sem.at[1, k], to)

    def mh_copy(k, i):
        peer = lax.rem(me + k, n)
        return remote(
            mh.at[peer // group], mh_slots.at[i], mh_sem.at[0, k], mh_sem.at[1, k], {"dp": peer}
        )

    @pl.loop(1, n)
    def _(k):
        t_copy(k, me).start()

    @pl.loop(1, n)
    def _(k):
        t_copy(k, before(k)).wait_recv()

    total = lax.fori_loop(0, n, lambda i, s: s + t_slots[i], zero)

    @pl.loop(0, p_rows // strip)
    def _(i):
        at = strip_of(i)
        slope = lists[9:10, :] * (1.0 / temperature)
        grads = slope * (raw_far[at, :] * (1.0 / total) - is_own(i))
        g_q[at, :] = (grads * p_scale(at)).astype(bf16)
        g_p[at, :] = (grads * q_scale()).astype(bf16)
        radial = temperature * jnp.sum(grads * raw[at, :], axis=1, keepdims=True)
        col[at, :] = jnp.broadcast_to(radial, (strip, tile))

    def owner(s):
        return lax.rem(a + s, na) * group + b

    def s1_copy(s, h, c):
        i = owner(s) + (dx if h else dy) + (dx + dy - (dx if h else dy)) * c
        return remote(
            bit(part, i, h),
            r1.at[s, h, c],
            s1_sem.at[0, s, 2 * h + c],
            s1_sem.at[1, s, 2 * h + c],
            xp if h else yp,
        )

    def s2_copy(s, h):
        i = owner(s) + (dy if h else dx)
        return remote(
            bit(part, i, h), r2.at[s, h], s2_sem.at[0, s, h], s2_sem.at[1, s, h], yp if h else xp
        )

    def s3_copy(s):
        i = owner(s)
        src = part.at[pl.ds(pl.multiple_of(i * rows, rows), rows), :]
        return remote(src, r3.at[s], s3_sem.at[0, s], s3_sem.at[1, s], {"dp": i})

    @pl.loop(0, na)
    def _(j):
        s = lax.rem(j + 1, na)
        at = pl.ds(pl.multiple_of(lax.rem(a + s, na) * tile, tile), tile)
        part[at, :] = dot(g_q[:, at], p_half[...], by_first).astype(bf16)
        for c in (1, 0):
            for h in range(2):
                s1_copy(s, h, c).start()

    @pl.loop(1, n)
    def _(k):
        mh_copy(k, me).start()

    for j in range(p_steps):
        at = slice(j * p_chunk, (j + 1) * p_chunk)
        grad = dot(g_p[...], q_all[:, at])
        inv = p_scale(slice(0, p_rows))
        p_dir[:, at] = (inv * (grad - p_proj[:, at] * (inv * col[:, 0:1]))).astype(bf16)

    out_chunk = p_send.shape[2]
    out_steps = half // out_chunk

    def back_rows(which, c):
        return pl.ds(pl.multiple_of(which * half + c * out_chunk, out_chunk), out_chunk)

    def p_copy(c):
        return remote(p_send.at[c], p_recv.at[c], back_sem.at[0, c], back_sem.at[1, c], other)

    def p_far(c):
        p_send[c] = dot(p_dir[...], w[back_rows(1 - core, c), :], by_rows).astype(bf16)
        p_copy(c).start()

    def first_sum(s, h):
        s1_copy(s, h, 0).wait_recv()
        s2_copy(s, h).wait_recv()
        mine = bit(part, owner(s), h)[...].astype(f32)
        return mine + r1[s, h, 0].astype(f32) + r2[s, h].astype(f32)

    @pl.loop(0, na)
    def _(j):
        s = lax.rem(j + 1, na)
        for h in range(2):
            s1_copy(s, h, 1).wait_recv()
            ref = bit(part, owner(s) + (dy if h else dx), h)
            ref[...] = (ref[...].astype(f32) + r1[s, h, 1].astype(f32)).astype(bf16)
            s2_copy(s, h).start()

        @pl.when(j < out_steps)
        def _():
            p_far(j)

        @pl.when(j >= 1)
        def _():
            for h in range(2):
                bit(part, owner(j), h)[...] = first_sum(j, h).astype(bf16)
            s3_copy(j).start()

    for c in range(na, out_steps):
        p_far(c)

    for h in range(2):
        q_grad[h * piece : (h + 1) * piece, :] = first_sum(0, h)

    def done_copy(c):
        at = pl.ds(pl.multiple_of(c * out_chunk, out_chunk), out_chunk)
        return pltpu.make_async_copy(p_done.at[c], p_out.at[:, at], done_sem.at[c])

    @pl.loop(0, out_steps)
    def _(c):
        kept = dot(p_dir[...], w[back_rows(core, c), :], by_rows)
        p_copy(c).wait_recv()
        p_done[c] = (kept + p_recv[c].astype(f32)).astype(bf16)
        done_copy(c).start()

    @pl.loop(1, n)
    def _(k):
        mh_copy(k, before(k)).wait_recv()

    sums = lax.fori_loop(0, n, lambda i, s: s + mh_slots[i], jnp.zeros((8, tile), f32))
    at = pl.ds(pl.multiple_of(a * tile, tile), tile)
    t_own = lax.fori_loop(
        0, n, lambda i, s: s + t_slots[i, :, at], jnp.zeros((1, tile), f32)
    )
    inv = lax.rsqrt(raw[p_rows : p_rows + 1, at] + raw_far[p_rows : p_rows + 1, at] + 1e-06)
    own_moment, own_hit = sums[0:1, :], sums[1:2, :]
    loss = jnp.log(t_own) - own_hit
    radial = lists[9:10, at] * (own_moment / t_own - own_hit)
    three = jnp.concatenate([loss, inv, inv * radial, jnp.zeros((5, tile), f32)], axis=0)
    turn[...] = jnp.concatenate([three] * (tile // 8), axis=0).T
    mine = turn[pl.ds(pl.multiple_of(b * rows, rows), rows), :]
    loss_ref[...] = pltpu.roll(three, lax.rem(tile - b * rows, tile), 1)[0:1, 0:rows]

    @pl.loop(1, na)
    def _(s):
        s3_copy(s).wait_recv()
        q_grad[...] += r3[s].astype(f32)

    q_dir = (mine[:, 1:2] * (q_grad[...] - q_proj[...] * mine[:, 2:3])).astype(bf16)
    qs[:, 0:width] = q_dir

    def q_copy(c):
        return remote(q_send.at[c], q_recv.at[c], q_sem.at[0, c], q_sem.at[1, c], other)

    @pl.loop(0, out_steps)
    def _(c):
        q_send[c] = dot(qs[:, 0:width], w[back_rows(1 - core, c), :], by_rows).astype(bf16)
        q_copy(c).start()

    @pl.loop(0, out_steps)
    def _(c):
        to = pl.ds(pl.multiple_of(c * out_chunk, out_chunk), out_chunk)
        kept = dot(qs[:, 0:width], w[back_rows(core, c), :], by_rows)
        q_copy(c).wait_recv()
        q_out[:, to] = (kept + q_recv[c].astype(f32)).astype(bf16)

    psq_copy.wait_send()

    @pl.loop(0, out_steps)
    def _(c):
        p_copy(c).wait_send()
        q_copy(c).wait_send()
        done_copy(c).wait()

    @pl.loop(1, n)
    def _(k):
        list_copy(k, me).wait_send()
        sq_copy(k, me).wait_send()
        t_copy(k, me).wait_send()
        mh_copy(k, me).wait_send()

    @pl.loop(0, na)
    def _(s):
        x_copy(s, column(s)).wait_send()
        y_copy(s, column(s)).wait_send()
        fy_copy(s, column(s) + dx).wait_send()
        fx_copy(s, column(s) + dy).wait_send()
        for h in range(2):
            s1_copy(s, h, 0).wait_send()
            s1_copy(s, h, 1).wait_send()
            s2_copy(s, h).wait_send()

    @pl.loop(1, na)
    def _(s):
        z_copy(s, me).wait_send()
        s3_copy(s).wait_send()


def hand_over(loss, q, p, loss_out, q_out, p_out, loss_buf, q_buf, p_buf, sems):
    parts = sems.shape[1] - 2
    size = p.shape[0] // parts
    routes = [(loss, loss_buf, loss_out), (q, q_buf, q_out)]
    for i in range(parts):
        at = slice(i * size, (i + 1) * size)
        routes.append((p.at[at, :], p_buf.at[at, :], p_out.at[at, :]))
    into = [pltpu.make_async_copy(x, y, sems.at[0, i]) for i, (x, y, _) in enumerate(routes)]
    away = [pltpu.make_async_copy(y, z, sems.at[1, i]) for i, (_, y, z) in enumerate(routes)]
    order = list(range(2, parts + 2)) + [0, 1]
    for i in order:
        into[i].start()
    for i in order:
        into[i].wait()
        away[i].start()
    for i in order:
        away[i].wait()


def per_device(
    n, query_states, passage_states, head_weight, positives, negatives, search_cost_incoming_slope
):
    rows, depth = query_states.shape
    p_rows = passage_states.shape[0]
    width = head_weight.shape[1]
    half = depth // 2
    queries = n * rows
    group = tile // rows
    na = n // group
    piece = rows // 2
    names = 1 + negatives.shape[1]
    steps = 4
    dma = pltpu.SemaphoreType.DMA
    vmem = pltpu.VMEM
    flops = 2 * width * (2 * (rows + p_rows) * depth + 3 * queries * p_rows)
    out = pl.pallas_call(
        functools.partial(kernel, n, names),
        out_shape=(
            jax.ShapeDtypeStruct((1, rows), f32),
            jax.ShapeDtypeStruct((rows, half), bf16),
            jax.ShapeDtypeStruct((p_rows, half), bf16),
        ),
        in_specs=[pl.BlockSpec(memory_space=pl.ANY)] * 3
        + [pl.BlockSpec(memory_space=pltpu.VMEM)] * 3,
        out_specs=[pl.BlockSpec(memory_space=pltpu.VMEM)] * 2
        + [pl.BlockSpec(memory_space=pl.ANY)],
        scratch_shapes=[
            vmem((rows, depth), bf16),
            vmem((p_rows, depth), bf16),
            vmem((depth, width), bf16),
            vmem((rows, width), f32),
            vmem((queries, width), bf16),
            vmem((p_rows, width), f32),
            vmem((p_rows, width), bf16),
            vmem((p_rows, width), bf16),
            vmem((n, 16, tile), f32),
            vmem((n, 1, tile), f32),
            vmem((16, queries), f32),
            vmem((p_rows, tile), f32),
            vmem((p_rows, tile), f32),
            vmem((p_rows, tile), f32),
            vmem((p_rows + 8, queries), f32),
            vmem((p_rows + 8, queries), f32),
            vmem((p_rows, queries), bf16),
            vmem((p_rows, queries), bf16),
            vmem((n, 1, queries), f32),
            vmem((na, 8, tile), f32),
            vmem((n, 8, tile), f32),
            vmem((tile, tile), f32),
            vmem((queries, width), bf16),
            vmem((na, 2, 2, piece, width), bf16),
            vmem((na, 2, piece, width), bf16),
            vmem((na, rows, width), bf16),
            vmem((rows, width), f32),
            vmem((steps, p_rows, half // steps), bf16),
            vmem((steps, p_rows, half // steps), bf16),
            vmem((steps, rows, half // steps), bf16),
            vmem((steps, rows, half // steps), bf16),
            vmem((steps, p_rows, half // steps), bf16),
            dma((w_parts + 2,)),
            dma((6,)),
            dma((2, 2)),
            dma((2, na)),
            dma((2, na)),
            dma((2, na)),
            dma((2, na)),
            dma((2, na)),
            dma((2, n)),
            dma((2, n)),
            dma((2, n)),
            dma((2, n)),
            dma((2, na, 4)),
            dma((2, na, 2)),
            dma((2, na)),
            dma((2, steps)),
            dma((2, steps)),
            dma((steps,)),
        ],
        compiler_params=pltpu.CompilerParams(
            collective_id=0, has_side_effects=True, vmem_limit_bytes=60 * 2**20
        ),
        cost_estimate=pl.CostEstimate(
            flops=flops, bytes_accessed=12 * 2**20, transcendentals=queries * p_rows
        ),
        name="contrastive",
    )(
        query_states,
        passage_states,
        head_weight,
        positives.reshape(1, rows),
        negatives.T,
        search_cost_incoming_slope.reshape(1, rows),
    )
    losses, q_rows, p_rows_out = pl.pallas_call(
        hand_over,
        out_shape=tuple(jax.ShapeDtypeStruct(x.shape, x.dtype) for x in out),
        in_specs=[pl.BlockSpec(memory_space=pl.ANY)] * 3,
        out_specs=[pl.BlockSpec(memory_space=pl.ANY)] * 3,
        scratch_shapes=[vmem(x.shape, x.dtype) for x in out] + [dma((2, 2 + steps))],
        compiler_params=pltpu.CompilerParams(vmem_limit_bytes=60 * 2**20),
        name="hand_over",
    )(*out)
    return losses.reshape(rows), q_rows, p_rows_out


def solution(mesh):
    placed = (P("dp", None), P("dp", None), P(None, "mp"), P("dp"), P("dp", None), P("dp"))
    return jax.shard_map(
        functools.partial(per_device, mesh.shape["dp"]),
        mesh=mesh,
        in_specs=placed,
        out_specs=(P("dp"), P("dp", "mp"), P("dp", "mp")),
        check_vma=False,
    )
```

```python
import functools

import jax
import jax.numpy as jnp
from jax import lax
from jax.experimental import pallas as pl
from jax.experimental.pallas import tpu as pltpu
from jax.sharding import PartitionSpec as P

temperature = 0.02
by_rows = (((1,), (1,)), ((), ()))
by_first = (((0,), (0,)), ((), ()))
f32 = jnp.float32
bf16 = jnp.bfloat16
tile = 128
w_parts = 8
window = 4
strip = 32
s_chunk = 512


def dot(x, y, dims=(((1,), (0,)), ((), ()))):
    return lax.dot_general(x, y, dims, preferred_element_type=f32)


def remote(src, dst, send, recv, where):
    return pltpu.make_async_remote_copy(
        src_ref=src,
        dst_ref=dst,
        send_sem=send,
        recv_sem=recv,
        device_id=where,
        device_id_type=pl.DeviceIdType.MESH,
    )


def kernel(
    n,
    names,
    q_hbm,
    p_hbm,
    w_hbm,
    pos_ref,
    neg_ref,
    slope_ref,
    loss_ref,
    q_out,
    p_out,
    qs,
    ps,
    w,
    q_proj,
    q_all,
    p_proj,
    p_half,
    p_dir,
    slots,
    sq_slots,
    lists,
    psq,
    psq_far,
    col,
    raw,
    raw_far,
    g_q,
    g_p,
    t_slots,
    mh,
    mh_slots,
    turn,
    part,
    r1,
    r2,
    r3,
    q_grad,
    p_send,
    p_recv,
    q_send,
    q_recv,
    p_done,
    load,
    pair,
    raw_sem,
    z_sem,
    x_sem,
    y_sem,
    fx_sem,
    fy_sem,
    list_sem,
    sq_sem,
    t_sem,
    mh_sem,
    s1_sem,
    s2_sem,
    s3_sem,
    back_sem,
    q_sem,
    done_sem,
):
    rows, depth = qs.shape
    p_rows, width = p_proj.shape
    queries = q_all.shape[0]
    piece = rows // 2
    group = tile // rows
    na = n // group
    half = depth // 2
    me = lax.axis_index("dp")
    core = lax.axis_index("mp")
    a, b = me // group, lax.rem(me, group)
    x, y = lax.rem(me, 2), lax.rem(me // 2, 2)
    dx, dy = 1 - 2 * x, 2 - 4 * y
    xp, yp, other = {"dp": me + dx}, {"dp": me + dy}, {"mp": 1 - core}

    k_rows = depth // w_parts

    def w_load(i):
        at = pl.ds(pl.multiple_of(i * k_rows, k_rows), k_rows)
        return pltpu.make_async_copy(w_hbm.at[at, :], w.at[at, :], load.at[i])

    q_load = pltpu.make_async_copy(q_hbm, qs, load.at[w_parts])
    p_load = pltpu.make_async_copy(p_hbm, ps, load.at[w_parts + 1])
    q_load.start()
    for i in range(window):
        w_load(i).start()

    barrier = pltpu.get_barrier_semaphore()

    @pl.loop(1, n)
    def _(k):
        pl.semaphore_signal(
            barrier,
            inc=1,
            device_id={"dp": lax.rem(me + k, n)},
            device_id_type=pl.DeviceIdType.MESH,
        )

    pl.semaphore_signal(
        barrier, inc=1, device_id=other, device_id_type=pl.DeviceIdType.MESH
    )

    def before(k):
        return lax.rem(me - k + n, n)

    def list_copy(k, i):
        to = {"dp": lax.rem(me + k, n)}
        return remote(slots.at[i], slots.at[i], list_sem.at[0, k], list_sem.at[1, k], to)

    def sq_copy(k, i):
        to = {"dp": lax.rem(me + k, n)}
        return remote(sq_slots.at[i], sq_slots.at[i], sq_sem.at[0, k], sq_sem.at[1, k], to)

    turn[0:24, :] = jnp.zeros((24, tile), f32)
    turn[0 : names - 1, 0:rows] = neg_ref[...].astype(f32)
    turn[8:9, 0:rows] = pos_ref[...].astype(f32)
    turn[16:17, 0:rows] = slope_ref[...]
    neg_lanes, pos_lanes, slope_lanes = [
        pltpu.roll(turn[8 * i : 8 * i + 8, :], b * rows, 1) for i in range(3)
    ]
    lane = lax.broadcasted_iota(jnp.int32, (1, tile), 1)
    mask = lane // rows == b
    slots[me] = jnp.concatenate(
        [
            pos_lanes[0:1, :],
            neg_lanes[0 : names - 1, :],
            slope_lanes[0:1, :],
            jnp.zeros((15 - names, tile), f32),
        ],
        axis=0,
    )
    pl.semaphore_wait(barrier, n)

    @pl.loop(1, n)
    def _(k):
        list_copy(k, me).start()

    q_load.wait()
    total = None
    for i in range(w_parts):
        w_load(i).wait()
        if i + window < w_parts:
            w_load(i + window).start()
        if i + window == w_parts:
            p_load.start()
        at = slice(i * k_rows, (i + 1) * k_rows)
        term = dot(qs[:, at], w[at, :])
        total = term if total is None else total + term
    q_proj[...] = total

    def block(i):
        return q_all.at[pl.ds(pl.multiple_of(i * rows, rows), rows), :]

    def bit(ref, i, h):
        return ref.at[pl.ds(pl.multiple_of(i * rows + h * piece, piece), piece), :]

    q_all[pl.ds(pl.multiple_of(me * rows, rows), rows), :] = q_proj[...].astype(bf16)
    def z_copy(s, i):
        to = {"dp": lax.rem(a + s, na) * group + b}
        return remote(block(i), block(i), z_sem.at[0, s], z_sem.at[1, s], to)

    def column(s):
        return lax.rem(a - s + na, na) * group + b

    def x_copy(s, i):
        return remote(block(i), block(i), x_sem.at[0, s], x_sem.at[1, s], xp)

    def y_copy(s, i):
        return remote(block(i), block(i), y_sem.at[0, s], y_sem.at[1, s], yp)

    def fx_copy(s, i):
        return remote(bit(q_all, i, 1), bit(q_all, i, 1), fx_sem.at[0, s], fx_sem.at[1, s], xp)

    def fy_copy(s, i):
        return remote(bit(q_all, i, 0), bit(q_all, i, 0), fy_sem.at[0, s], fy_sem.at[1, s], yp)

    @pl.loop(1, na)
    def _(s):
        z_copy(s, me).start()

    x_copy(0, me).start()
    y_copy(0, me).start()

    q_square = jnp.sum(q_proj[...] * q_proj[...], axis=1, keepdims=True)
    square_rows = jnp.broadcast_to(q_square, (rows, tile))
    square_lanes = jnp.concatenate([square_rows] * group, axis=0).T
    sq_slots[me] = jnp.where(mask, square_lanes[0:1, :], 0.0)

    @pl.loop(1, n)
    def _(k):
        sq_copy(k, me).start()

    p_load.wait()
    p_chunk = 256
    p_steps = width // p_chunk
    psq[...] = jnp.zeros_like(psq)
    for j in range(p_steps):
        at = slice(j * p_chunk, (j + 1) * p_chunk)
        out = dot(ps[...], w[:, at])
        p_proj[:, at] = out
        p_half[:, at] = out.astype(bf16)
        psq[...] += jnp.broadcast_to(jnp.sum(out * out, axis=1, keepdims=True), psq.shape)
        lo = 1 + j * (na - 1) // p_steps
        hi = 1 + (j + 1) * (na - 1) // p_steps

        @pl.loop(lo, hi)
        def _(s):
            z_copy(s, column(s)).wait_recv()
            x_copy(s, column(s)).start()
            y_copy(s, column(s)).start()

    psq_copy = remote(psq, psq_far, pair.at[0], pair.at[1], other)
    psq_copy.start()

    @pl.loop(0, na)
    def _(s):
        x_copy(s, column(s) + dx).wait_recv()
        fy_copy(s, column(s) + dx).start()
        y_copy(s, column(s) + dy).wait_recv()
        fx_copy(s, column(s) + dy).start()

    @pl.loop(1, n)
    def _(k):
        list_copy(k, before(k)).wait_recv()
        sq_copy(k, before(k)).wait_recv()

    @pl.loop(0, na)
    def _(t):
        at = pl.ds(pl.multiple_of(t * tile, tile), tile)
        full, square = slots[t * group], sq_slots[t * group]
        for g in range(1, group):
            full = full + slots[t * group + g]
            square = square + sq_slots[t * group + g]
        lists[:, at] = full
        raw[p_rows : p_rows + 8, at] = jnp.broadcast_to(square, (8, tile))

    def strip_of(i):
        return pl.ds(pl.multiple_of(i * strip, strip), strip)

    def numbers_of(i):
        first = me * p_rows + i * strip
        return (first + lax.broadcasted_iota(jnp.int32, (strip, 1), 0)).astype(f32)

    def is_own(i):
        return (lists[0:1, :] == numbers_of(i)).astype(f32)

    @pl.loop(0, p_rows // strip)
    def _(i):
        numbers = numbers_of(i)
        named = jnp.sum(is_own(i), axis=1, keepdims=True)
        col[strip_of(i), :] = jnp.broadcast_to(named, (strip, tile))
        times = (lists[1:2, :] == numbers).astype(f32)
        for k in range(2, names):
            times = times + (lists[k : k + 1, :] == numbers).astype(f32)
        g_q[strip_of(i), :] = times.astype(bf16)

    psq_copy.wait_recv()

    @pl.loop(0, na)
    def _(s):
        fx_copy(s, column(s) + dx + dy).wait_recv()
        fy_copy(s, column(s) + dx + dy).wait_recv()

    s_rows = p_rows // 2
    sq_far_copy = remote(
        raw.at[p_rows : p_rows + 8, :], raw_far.at[p_rows : p_rows + 8, :], pair.at[4], pair.at[5], other
    )
    sq_far_copy.start()

    def raw_copy(i):
        at = pl.ds(pl.multiple_of(i * s_rows, s_rows), s_rows)
        return remote(raw.at[at, :], raw_far.at[at, :], raw_sem.at[0, i], raw_sem.at[1, i], other)

    for i in range(2):
        at = slice(i * s_rows, (i + 1) * s_rows)
        for j in range(queries // s_chunk):
            to = slice(j * s_chunk, (j + 1) * s_chunk)
            raw[at, to] = dot(p_half[at, :], q_all[to, :], by_rows)
        raw_copy(i).start()

    sq_far_copy.wait()

    def q_scale():
        return lax.rsqrt(raw[p_rows : p_rows + 1, :] + raw_far[p_rows : p_rows + 1, :] + 1e-06)

    def p_scale(at):
        return lax.rsqrt(psq[at, 0:1] + psq_far[at, 0:1] + 1e-06)

    zero = jnp.zeros((1, queries), f32)

    def score_strip(i, sums):
        at = strip_of(i)
        scores = (raw[at, :] + raw_far[at, :]) * (q_scale() * (1.0 / temperature)) * p_scale(at)
        powers = (col[at, 0:1] + g_q[at, :].astype(f32)) * jnp.exp(scores)
        raw[at, :] = scores
        raw_far[at, :] = powers
        new = (powers, powers * scores, is_own(i) * scores)
        return tuple(s + jnp.sum(v, axis=0, keepdims=True) for s, v in zip(sums, new))

    sums = (zero, zero, zero)
    s_strips = s_rows // strip
    for i in range(2):
        raw_copy(i).wait()
        sums = lax.fori_loop(i * s_strips, (i + 1) * s_strips, score_strip, sums)
    total, moment, hit = sums

    t_slots[me] = total
    for t in range(na):
        at = slice(t * tile, (t + 1) * tile)
        mh[t] = jnp.concatenate([moment[:, at], hit[:, at], jnp.zeros((6, tile), f32)], axis=0)
    mh_slots[me] = mh[a]

    def t_copy(k, i):
        to = {"dp": lax.rem(me + k, n)}
        return remote(t_slots.at[i], t_slots.at[i], t_sem.at[0, k], t_sem.at[1, k], to)

    def mh_copy(k, i):
        peer = lax.rem(me + k, n)
        return remote(
            mh.at[peer // group], mh_slots.at[i], mh_sem.at[0, k], mh_sem.at[1, k], {"dp": peer}
        )

    @pl.loop(1, n)
    def _(k):
        t_copy(k, me).start()

    @pl.loop(1, n)
    def _(k):
        t_copy(k, before(k)).wait_recv()

    total = lax.fori_loop(0, n, lambda i, s: s + t_slots[i], zero)

    @pl.loop(0, p_rows // strip)
    def _(i):
        at = strip_of(i)
        slope = lists[9:10, :] * (1.0 / temperature)
        grads = slope * (raw_far[at, :] * (1.0 / total) - is_own(i))
        g_q[at, :] = (grads * p_scale(at)).astype(bf16)
        g_p[at, :] = (grads * q_scale()).astype(bf16)
        radial = temperature * jnp.sum(grads * raw[at, :], axis=1, keepdims=True)
        col[at, :] = jnp.broadcast_to(radial, (strip, tile))

    def owner(s):
        return lax.rem(a + s, na) * group + b

    def s1_copy(s, h, c):
        i = owner(s) + (dx if h else dy) + (dx + dy - (dx if h else dy)) * c
        return remote(
            bit(part, i, h),
            r1.at[s, h, c],
            s1_sem.at[0, s, 2 * h + c],
            s1_sem.at[1, s, 2 * h + c],
            xp if h else yp,
        )

    def s2_copy(s, h):
        i = owner(s) + (dy if h else dx)
        return remote(
            bit(part, i, h), r2.at[s, h], s2_sem.at[0, s, h], s2_sem.at[1, s, h], yp if h else xp
        )

    def s3_copy(s):
        i = owner(s)
        src = part.at[pl.ds(pl.multiple_of(i * rows, rows), rows), :]
        return remote(src, r3.at[s], s3_sem.at[0, s], s3_sem.at[1, s], {"dp": i})

    @pl.loop(0, na)
    def _(j):
        s = lax.rem(j + 1, na)
        at = pl.ds(pl.multiple_of(lax.rem(a + s, na) * tile, tile), tile)
        part[at, :] = dot(g_q[:, at], p_half[...], by_first).astype(bf16)
        for c in (1, 0):
            for h in range(2):
                s1_copy(s, h, c).start()

    @pl.loop(1, n)
    def _(k):
        mh_copy(k, me).start()

    for j in range(p_steps):
        at = slice(j * p_chunk, (j + 1) * p_chunk)
        grad = dot(g_p[...], q_all[:, at])
        inv = p_scale(slice(0, p_rows))
        p_dir[:, at] = (inv * (grad - p_proj[:, at] * (inv * col[:, 0:1]))).astype(bf16)

    out_chunk = p_send.shape[2]
    out_steps = half // out_chunk

    def back_rows(which, c):
        return pl.ds(pl.multiple_of(which * half + c * out_chunk, out_chunk), out_chunk)

    def p_copy(c):
        return remote(p_send.at[c], p_recv.at[c], back_sem.at[0, c], back_sem.at[1, c], other)

    def p_far(c):
        p_send[c] = dot(p_dir[...], w[back_rows(1 - core, c), :], by_rows).astype(bf16)
        p_copy(c).start()

    def first_sum(s, h):
        s1_copy(s, h, 0).wait_recv()
        s2_copy(s, h).wait_recv()
        mine = bit(part, owner(s), h)[...].astype(f32)
        return mine + r1[s, h, 0].astype(f32) + r2[s, h].astype(f32)

    @pl.loop(0, na)
    def _(j):
        s = lax.rem(j + 1, na)
        for h in range(2):
            s1_copy(s, h, 1).wait_recv()
            ref = bit(part, owner(s) + (dy if h else dx), h)
            ref[...] = (ref[...].astype(f32) + r1[s, h, 1].astype(f32)).astype(bf16)
            s2_copy(s, h).start()

        @pl.when(j < out_steps)
        def _():
            p_far(j)

        @pl.when(j >= 1)
        def _():
            for h in range(2):
                bit(part, owner(j), h)[...] = first_sum(j, h).astype(bf16)
            s3_copy(j).start()

    for c in range(na, out_steps):
        p_far(c)

    for h in range(2):
        q_grad[h * piece : (h + 1) * piece, :] = first_sum(0, h)

    def done_copy(c):
        at = pl.ds(pl.multiple_of(c * out_chunk, out_chunk), out_chunk)
        return pltpu.make_async_copy(p_done.at[c], p_out.at[:, at], done_sem.at[c])

    @pl.loop(0, out_steps)
    def _(c):
        kept = dot(p_dir[...], w[back_rows(core, c), :], by_rows)
        p_copy(c).wait_recv()
        p_done[c] = (kept + p_recv[c].astype(f32)).astype(bf16)
        done_copy(c).start()

    @pl.loop(1, n)
    def _(k):
        mh_copy(k, before(k)).wait_recv()

    sums = lax.fori_loop(0, n, lambda i, s: s + mh_slots[i], jnp.zeros((8, tile), f32))
    at = pl.ds(pl.multiple_of(a * tile, tile), tile)
    t_own = lax.fori_loop(
        0, n, lambda i, s: s + t_slots[i, :, at], jnp.zeros((1, tile), f32)
    )
    inv = lax.rsqrt(raw[p_rows : p_rows + 1, at] + raw_far[p_rows : p_rows + 1, at] + 1e-06)
    own_moment, own_hit = sums[0:1, :], sums[1:2, :]
    loss = jnp.log(t_own) - own_hit
    radial = lists[9:10, at] * (own_moment / t_own - own_hit)
    three = jnp.concatenate([loss, inv, inv * radial, jnp.zeros((5, tile), f32)], axis=0)
    turn[...] = jnp.concatenate([three] * (tile // 8), axis=0).T
    mine = turn[pl.ds(pl.multiple_of(b * rows, rows), rows), :]
    loss_ref[...] = pltpu.roll(three, lax.rem(tile - b * rows, tile), 1)[0:1, 0:rows]

    @pl.loop(1, na)
    def _(s):
        s3_copy(s).wait_recv()
        q_grad[...] += r3[s].astype(f32)

    q_dir = (mine[:, 1:2] * (q_grad[...] - q_proj[...] * mine[:, 2:3])).astype(bf16)

    def q_copy(c):
        return remote(q_send.at[c], q_recv.at[c], q_sem.at[0, c], q_sem.at[1, c], other)

    q_chunk = q_send.shape[2]
    q_steps = half // q_chunk

    def q_back(which, c):
        at = pl.ds(pl.multiple_of(which * half + c * q_chunk, q_chunk), q_chunk)
        return dot(q_dir, w[at, :], by_rows)

    for c in range(q_steps):
        q_send[c] = q_back(1 - core, c).astype(bf16)
        q_copy(c).start()
    for c in range(q_steps):
        kept = q_back(core, c)
        q_copy(c).wait_recv()
        q_out[:, c * q_chunk : (c + 1) * q_chunk] = (kept + q_recv[c].astype(f32)).astype(bf16)

    psq_copy.wait_send()
    for c in range(q_steps):
        q_copy(c).wait_send()

    @pl.loop(0, out_steps)
    def _(c):
        p_copy(c).wait_send()
        done_copy(c).wait()

    @pl.loop(1, n)
    def _(k):
        list_copy(k, me).wait_send()
        sq_copy(k, me).wait_send()
        t_copy(k, me).wait_send()
        mh_copy(k, me).wait_send()

    @pl.loop(0, na)
    def _(s):
        x_copy(s, column(s)).wait_send()
        y_copy(s, column(s)).wait_send()
        fy_copy(s, column(s) + dx).wait_send()
        fx_copy(s, column(s) + dy).wait_send()
        for h in range(2):
            s1_copy(s, h, 0).wait_send()
            s1_copy(s, h, 1).wait_send()
            s2_copy(s, h).wait_send()

    @pl.loop(1, na)
    def _(s):
        z_copy(s, me).wait_send()
        s3_copy(s).wait_send()


def hand_over(loss, q, p, loss_out, q_out, p_out, loss_buf, q_buf, p_buf, sems):
    parts = sems.shape[1] - 2
    size = p.shape[0] // parts
    routes = [(loss, loss_buf, loss_out), (q, q_buf, q_out)]
    for i in range(parts):
        at = slice(i * size, (i + 1) * size)
        routes.append((p.at[at, :], p_buf.at[at, :], p_out.at[at, :]))
    into = [pltpu.make_async_copy(x, y, sems.at[0, i]) for i, (x, y, _) in enumerate(routes)]
    away = [pltpu.make_async_copy(y, z, sems.at[1, i]) for i, (_, y, z) in enumerate(routes)]
    order = list(range(2, parts + 2)) + [0, 1]
    for i in order:
        into[i].start()
    for i in order:
        into[i].wait()
        away[i].start()
    for i in order:
        away[i].wait()


def per_device(
    n, query_states, passage_states, head_weight, positives, negatives, search_cost_incoming_slope
):
    rows, depth = query_states.shape
    p_rows = passage_states.shape[0]
    width = head_weight.shape[1]
    half = depth // 2
    queries = n * rows
    group = tile // rows
    na = n // group
    piece = rows // 2
    names = 1 + negatives.shape[1]
    steps = 4
    dma = pltpu.SemaphoreType.DMA
    vmem = pltpu.VMEM
    flops = 2 * width * (2 * (rows + p_rows) * depth + 3 * queries * p_rows)
    out = pl.pallas_call(
        functools.partial(kernel, n, names),
        out_shape=(
            jax.ShapeDtypeStruct((1, rows), f32),
            jax.ShapeDtypeStruct((rows, half), bf16),
            jax.ShapeDtypeStruct((p_rows, half), bf16),
        ),
        in_specs=[pl.BlockSpec(memory_space=pl.ANY)] * 3
        + [pl.BlockSpec(memory_space=pltpu.VMEM)] * 3,
        out_specs=[pl.BlockSpec(memory_space=pltpu.VMEM)] * 2
        + [pl.BlockSpec(memory_space=pl.ANY)],
        scratch_shapes=[
            vmem((rows, depth), bf16),
            vmem((p_rows, depth), bf16),
            vmem((depth, width), bf16),
            vmem((rows, width), f32),
            vmem((queries, width), bf16),
            vmem((p_rows, width), f32),
            vmem((p_rows, width), bf16),
            vmem((p_rows, width), bf16),
            vmem((n, 16, tile), f32),
            vmem((n, 1, tile), f32),
            vmem((16, queries), f32),
            vmem((p_rows, tile), f32),
            vmem((p_rows, tile), f32),
            vmem((p_rows, tile), f32),
            vmem((p_rows + 8, queries), f32),
            vmem((p_rows + 8, queries), f32),
            vmem((p_rows, queries), bf16),
            vmem((p_rows, queries), bf16),
            vmem((n, 1, queries), f32),
            vmem((na, 8, tile), f32),
            vmem((n, 8, tile), f32),
            vmem((tile, tile), f32),
            vmem((queries, width), bf16),
            vmem((na, 2, 2, piece, width), bf16),
            vmem((na, 2, piece, width), bf16),
            vmem((na, rows, width), bf16),
            vmem((rows, width), f32),
            vmem((steps, p_rows, half // steps), bf16),
            vmem((steps, p_rows, half // steps), bf16),
            vmem((2, rows, half // 2), bf16),
            vmem((2, rows, half // 2), bf16),
            vmem((steps, p_rows, half // steps), bf16),
            dma((w_parts + 2,)),
            dma((6,)),
            dma((2, 2)),
            dma((2, na)),
            dma((2, na)),
            dma((2, na)),
            dma((2, na)),
            dma((2, na)),
            dma((2, n)),
            dma((2, n)),
            dma((2, n)),
            dma((2, n)),
            dma((2, na, 4)),
            dma((2, na, 2)),
            dma((2, na)),
            dma((2, steps)),
            dma((2, 2)),
            dma((steps,)),
        ],
        compiler_params=pltpu.CompilerParams(
            collective_id=0, has_side_effects=True, vmem_limit_bytes=63 * 2**20
        ),
        cost_estimate=pl.CostEstimate(
            flops=flops, bytes_accessed=12 * 2**20, transcendentals=queries * p_rows
        ),
        name="contrastive",
    )(
        query_states,
        passage_states,
        head_weight,
        positives.reshape(1, rows),
        negatives.T,
        search_cost_incoming_slope.reshape(1, rows),
    )
    losses, q_rows, p_rows_out = pl.pallas_call(
        hand_over,
        out_shape=tuple(jax.ShapeDtypeStruct(x.shape, x.dtype) for x in out),
        in_specs=[pl.BlockSpec(memory_space=pl.ANY)] * 3,
        out_specs=[pl.BlockSpec(memory_space=pl.ANY)] * 3,
        scratch_shapes=[vmem(x.shape, x.dtype) for x in out] + [dma((2, 2 + steps))],
        compiler_params=pltpu.CompilerParams(vmem_limit_bytes=60 * 2**20),
        name="hand_over",
    )(*out)
    return losses.reshape(rows), q_rows, p_rows_out


def solution(mesh):
    placed = (P("dp", None), P("dp", None), P(None, "mp"), P("dp"), P("dp", None), P("dp"))
    return jax.shard_map(
        functools.partial(per_device, mesh.shape["dp"]),
        mesh=mesh,
        in_specs=placed,
        out_specs=(P("dp"), P("dp", "mp"), P("dp", "mp")),
        check_vma=False,
    )
```

```python
import functools

import jax
import jax.numpy as jnp
from jax import lax
from jax.experimental import pallas as pl
from jax.experimental.pallas import tpu as pltpu
from jax.sharding import PartitionSpec as P

temperature = 0.02
by_rows = (((1,), (1,)), ((), ()))
by_first = (((0,), (0,)), ((), ()))
f32 = jnp.float32
bf16 = jnp.bfloat16
tile = 128
w_parts = 8
window = 4
strip = 32
s_chunk = 512


def dot(x, y, dims=(((1,), (0,)), ((), ()))):
    return lax.dot_general(x, y, dims, preferred_element_type=f32)


def remote(src, dst, send, recv, where):
    return pltpu.make_async_remote_copy(
        src_ref=src,
        dst_ref=dst,
        send_sem=send,
        recv_sem=recv,
        device_id=where,
        device_id_type=pl.DeviceIdType.MESH,
    )


def kernel(
    n,
    names,
    q_hbm,
    p_hbm,
    w_hbm,
    pos_ref,
    neg_ref,
    slope_ref,
    loss_ref,
    q_out,
    p_out,
    qs,
    ps,
    w,
    q_proj,
    q_all,
    p_proj,
    p_half,
    p_dir,
    slots,
    sq_slots,
    lists,
    psq,
    psq_far,
    col,
    raw,
    raw_far,
    g_q,
    g_p,
    t_slots,
    mh,
    mh_slots,
    turn,
    part,
    r1,
    r2,
    r3,
    q_grad,
    p_send,
    p_recv,
    q_send,
    q_recv,
    p_done,
    load,
    pair,
    raw_sem,
    z_sem,
    first_sem,
    then_sem,
    list_sem,
    sq_sem,
    t_sem,
    mh_sem,
    s1_sem,
    s2_sem,
    s3_sem,
    back_sem,
    q_sem,
    done_sem,
):
    rows, depth = qs.shape
    p_rows, width = p_proj.shape
    queries, wide = q_all.shape[1:]
    piece = rows // 2
    group = tile // rows
    na = n // group
    half = depth // 2
    me = lax.axis_index("dp")
    core = lax.axis_index("mp")
    a, b = me // group, lax.rem(me, group)
    x, y = lax.rem(me, 2), lax.rem(me // 2, 2)
    dx, dy = 1 - 2 * x, 2 - 4 * y
    xp, yp, other = {"dp": me + dx}, {"dp": me + dy}, {"mp": 1 - core}

    k_parts = w_parts // 2
    k_rows = depth // k_parts

    def w_load(i):
        at = slice(i % k_parts * k_rows, (i % k_parts + 1) * k_rows)
        to = slice(i // k_parts * wide, (i // k_parts + 1) * wide)
        return pltpu.make_async_copy(w_hbm.at[at, to], w.at[at, to], load.at[i])

    q_load = pltpu.make_async_copy(q_hbm, qs, load.at[w_parts])
    p_load = pltpu.make_async_copy(p_hbm, ps, load.at[w_parts + 1])
    q_load.start()
    for i in range(window):
        w_load(i).start()

    barrier = pltpu.get_barrier_semaphore()

    @pl.loop(1, n)
    def _(k):
        pl.semaphore_signal(
            barrier,
            inc=1,
            device_id={"dp": lax.rem(me + k, n)},
            device_id_type=pl.DeviceIdType.MESH,
        )

    pl.semaphore_signal(
        barrier, inc=1, device_id=other, device_id_type=pl.DeviceIdType.MESH
    )

    def before(k):
        return lax.rem(me - k + n, n)

    def list_copy(k, i):
        to = {"dp": lax.rem(me + k, n)}
        return remote(slots.at[i], slots.at[i], list_sem.at[0, k], list_sem.at[1, k], to)

    def sq_copy(k, i):
        to = {"dp": lax.rem(me + k, n)}
        return remote(sq_slots.at[i], sq_slots.at[i], sq_sem.at[0, k], sq_sem.at[1, k], to)

    turn[0:24, :] = jnp.zeros((24, tile), f32)
    turn[0 : names - 1, 0:rows] = neg_ref[...].astype(f32)
    turn[8:9, 0:rows] = pos_ref[...].astype(f32)
    turn[16:17, 0:rows] = slope_ref[...]
    neg_lanes, pos_lanes, slope_lanes = [
        pltpu.roll(turn[8 * i : 8 * i + 8, :], b * rows, 1) for i in range(3)
    ]
    lane = lax.broadcasted_iota(jnp.int32, (1, tile), 1)
    mask = lane // rows == b
    slots[me] = jnp.concatenate(
        [
            pos_lanes[0:1, :],
            neg_lanes[0 : names - 1, :],
            slope_lanes[0:1, :],
            jnp.zeros((15 - names, tile), f32),
        ],
        axis=0,
    )
    pl.semaphore_wait(barrier, n)

    @pl.loop(1, n)
    def _(k):
        list_copy(k, me).start()

    hop = ((xp, dx), (yp, dy))

    def block(h, i):
        return q_all.at[h, pl.ds(pl.multiple_of(i * rows, rows), rows), :]

    def column(s):
        return lax.rem(a - s + na, na) * group + b

    def z_copy(h, s, i):
        to = {"dp": lax.rem(a + s, na) * group + b}
        return remote(block(h, i), block(h, i), z_sem.at[0, h, s], z_sem.at[1, h, s], to)

    def first_copy(h, s, i):
        return remote(
            block(h, i), block(h, i), first_sem.at[0, h, s], first_sem.at[1, h, s], hop[h][0]
        )

    def then_copy(h, s, c, i):
        return remote(
            block(h, i), block(h, i), then_sem.at[0, h, s, c], then_sem.at[1, h, s, c], hop[1 - h][0]
        )

    def hand_on(s):
        for h in range(2):
            i = column(s) + hop[h][1]
            first_copy(h, s, i).wait_recv()
            then_copy(h, s, 1, i).start()

    q_load.wait()
    for h in range(2):
        total = None
        for i in range(h * k_parts, (h + 1) * k_parts):
            w_load(i).wait()
            if i + window < w_parts:
                w_load(i + window).start()
            if i + window == w_parts:
                p_load.start()
            at = slice(i % k_parts * k_rows, (i % k_parts + 1) * k_rows)
            term = dot(qs[:, at], w[at, h * wide : (h + 1) * wide])
            total = term if total is None else total + term
        q_proj[:, h * wide : (h + 1) * wide] = total
        q_all[h, pl.ds(pl.multiple_of(me * rows, rows), rows), :] = total.astype(bf16)
        first_copy(h, 0, me).start()

        @pl.loop(1, na)
        def _(s):
            z_copy(h, s, me).start()

        then_copy(h, 0, 0, me).start()

    q_square = jnp.sum(q_proj[...] * q_proj[...], axis=1, keepdims=True)
    square_rows = jnp.broadcast_to(q_square, (rows, tile))
    square_lanes = jnp.concatenate([square_rows] * group, axis=0).T
    sq_slots[me] = jnp.where(mask, square_lanes[0:1, :], 0.0)

    @pl.loop(1, n)
    def _(k):
        sq_copy(k, me).start()

    p_load.wait()
    p_chunk = 256
    p_steps = width // p_chunk
    psq[...] = jnp.zeros_like(psq)
    for j in range(p_steps):
        at = slice(j * p_chunk, (j + 1) * p_chunk)
        out = dot(ps[...], w[:, at])
        p_proj[:, at] = out
        p_half[:, at] = out.astype(bf16)
        psq[...] += jnp.broadcast_to(jnp.sum(out * out, axis=1, keepdims=True), psq.shape)
        lo = 1 + -(-j * (na - 1) // p_steps)
        hi = 1 + -(-(j + 1) * (na - 1) // p_steps)

        @pl.loop(lo, hi)
        def _(s):
            hand_on(s - 1)
            for h in range(2):
                z_copy(h, s, column(s)).wait_recv()
                first_copy(h, s, column(s)).start()
                then_copy(h, s, 0, column(s)).start()

    psq_copy = remote(psq, psq_far, pair.at[0], pair.at[1], other)
    psq_copy.start()

    hand_on(na - 1)

    @pl.loop(1, n)
    def _(k):
        list_copy(k, before(k)).wait_recv()
        sq_copy(k, before(k)).wait_recv()

    @pl.loop(0, na)
    def _(t):
        at = pl.ds(pl.multiple_of(t * tile, tile), tile)
        full, square = slots[t * group], sq_slots[t * group]
        for g in range(1, group):
            full = full + slots[t * group + g]
            square = square + sq_slots[t * group + g]
        lists[:, at] = full
        raw[p_rows : p_rows + 8, at] = jnp.broadcast_to(square, (8, tile))

    def strip_of(i):
        return pl.ds(pl.multiple_of(i * strip, strip), strip)

    def numbers_of(i):
        first = me * p_rows + i * strip
        return (first + lax.broadcasted_iota(jnp.int32, (strip, 1), 0)).astype(f32)

    def is_own(i):
        return (lists[0:1, :] == numbers_of(i)).astype(f32)

    @pl.loop(0, p_rows // strip)
    def _(i):
        numbers = numbers_of(i)
        named = jnp.sum(is_own(i), axis=1, keepdims=True)
        col[strip_of(i), :] = jnp.broadcast_to(named, (strip, tile))
        times = (lists[1:2, :] == numbers).astype(f32)
        for k in range(2, names):
            times = times + (lists[k : k + 1, :] == numbers).astype(f32)
        g_q[strip_of(i), :] = times.astype(bf16)

    psq_copy.wait_recv()

    @pl.loop(0, na)
    def _(s):
        for h in range(2):
            then_copy(h, s, 0, column(s) + hop[1 - h][1]).wait_recv()
            then_copy(h, s, 1, column(s) + dx + dy).wait_recv()

    s_rows = p_rows // 2
    sq_far_copy = remote(
        raw.at[p_rows : p_rows + 8, :], raw_far.at[p_rows : p_rows + 8, :], pair.at[4], pair.at[5], other
    )
    sq_far_copy.start()

    def raw_copy(i):
        at = pl.ds(pl.multiple_of(i * s_rows, s_rows), s_rows)
        return remote(raw.at[at, :], raw_far.at[at, :], raw_sem.at[0, i], raw_sem.at[1, i], other)

    for i in range(2):
        at = slice(i * s_rows, (i + 1) * s_rows)
        for j in range(queries // s_chunk):
            to = slice(j * s_chunk, (j + 1) * s_chunk)
            raw[at, to] = dot(p_half[at, 0:wide], q_all[0, to, :], by_rows) + dot(
                p_half[at, wide:], q_all[1, to, :], by_rows
            )
        raw_copy(i).start()

    sq_far_copy.wait()

    def q_scale():
        return lax.rsqrt(raw[p_rows : p_rows + 1, :] + raw_far[p_rows : p_rows + 1, :] + 1e-06)

    def p_scale(at):
        return lax.rsqrt(psq[at, 0:1] + psq_far[at, 0:1] + 1e-06)

    zero = jnp.zeros((1, queries), f32)

    def score_strip(i, sums):
        at = strip_of(i)
        scores = (raw[at, :] + raw_far[at, :]) * (q_scale() * (1.0 / temperature)) * p_scale(at)
        powers = (col[at, 0:1] + g_q[at, :].astype(f32)) * jnp.exp(scores)
        raw[at, :] = scores
        raw_far[at, :] = powers
        new = (powers, powers * scores, is_own(i) * scores)
        return tuple(s + jnp.sum(v, axis=0, keepdims=True) for s, v in zip(sums, new))

    sums = (zero, zero, zero)
    s_strips = s_rows // strip
    for i in range(2):
        raw_copy(i).wait()
        sums = lax.fori_loop(i * s_strips, (i + 1) * s_strips, score_strip, sums)
    total, moment, hit = sums

    t_slots[me] = total
    for t in range(na):
        at = slice(t * tile, (t + 1) * tile)
        mh[t] = jnp.concatenate([moment[:, at], hit[:, at], jnp.zeros((6, tile), f32)], axis=0)
    mh_slots[me] = mh[a]

    def t_copy(k, i):
        to = {"dp": lax.rem(me + k, n)}
        return remote(t_slots.at[i], t_slots.at[i], t_sem.at[0, k], t_sem.at[1, k], to)

    def mh_copy(k, i):
        peer = lax.rem(me + k, n)
        return remote(
            mh.at[peer // group], mh_slots.at[i], mh_sem.at[0, k], mh_sem.at[1, k], {"dp": peer}
        )

    @pl.loop(1, n)
    def _(k):
        t_copy(k, me).start()

    @pl.loop(1, n)
    def _(k):
        t_copy(k, before(k)).wait_recv()

    total = lax.fori_loop(0, n, lambda i, s: s + t_slots[i], zero)

    @pl.loop(0, p_rows // strip)
    def _(i):
        at = strip_of(i)
        slope = lists[9:10, :] * (1.0 / temperature)
        grads = slope * (raw_far[at, :] * (1.0 / total) - is_own(i))
        g_q[at, :] = (grads * p_scale(at)).astype(bf16)
        g_p[at, :] = (grads * q_scale()).astype(bf16)
        radial = temperature * jnp.sum(grads * raw[at, :], axis=1, keepdims=True)
        col[at, :] = jnp.broadcast_to(radial, (strip, tile))

    def bit(ref, i, h):
        return ref.at[pl.ds(pl.multiple_of(i * rows + h * piece, piece), piece), :]

    def owner(s):
        return lax.rem(a + s, na) * group + b

    def s1_copy(s, h, c):
        i = owner(s) + (dx if h else dy) + (dx + dy - (dx if h else dy)) * c
        return remote(
            bit(part, i, h),
            r1.at[s, h, c],
            s1_sem.at[0, s, 2 * h + c],
            s1_sem.at[1, s, 2 * h + c],
            xp if h else yp,
        )

    def s2_copy(s, h):
        i = owner(s) + (dy if h else dx)
        return remote(
            bit(part, i, h), r2.at[s, h], s2_sem.at[0, s, h], s2_sem.at[1, s, h], yp if h else xp
        )

    def s3_copy(s):
        i = owner(s)
        src = part.at[pl.ds(pl.multiple_of(i * rows, rows), rows), :]
        return remote(src, r3.at[s], s3_sem.at[0, s], s3_sem.at[1, s], {"dp": i})

    @pl.loop(0, na)
    def _(j):
        s = lax.rem(j + 1, na)
        at = pl.ds(pl.multiple_of(lax.rem(a + s, na) * tile, tile), tile)
        part[at, :] = dot(g_q[:, at], p_half[...], by_first).astype(bf16)
        for c in (1, 0):
            for h in range(2):
                s1_copy(s, h, c).start()

    @pl.loop(1, n)
    def _(k):
        mh_copy(k, me).start()

    for j in range(p_steps):
        at = slice(j * p_chunk, (j + 1) * p_chunk)
        h = j * p_chunk // wide
        grad = dot(g_p[...], q_all[h, :, j * p_chunk - h * wide : (j + 1) * p_chunk - h * wide])
        inv = p_scale(slice(0, p_rows))
        p_dir[:, at] = (inv * (grad - p_proj[:, at] * (inv * col[:, 0:1]))).astype(bf16)

    out_chunk = p_send.shape[2]
    out_steps = half // out_chunk

    def back_rows(which, c):
        return pl.ds(pl.multiple_of(which * half + c * out_chunk, out_chunk), out_chunk)

    def p_copy(c):
        return remote(p_send.at[c], p_recv.at[c], back_sem.at[0, c], back_sem.at[1, c], other)

    def p_far(c):
        p_send[c] = dot(p_dir[...], w[back_rows(1 - core, c), :], by_rows).astype(bf16)
        p_copy(c).start()

    def first_sum(s, h):
        s1_copy(s, h, 0).wait_recv()
        s2_copy(s, h).wait_recv()
        mine = bit(part, owner(s), h)[...].astype(f32)
        return mine + r1[s, h, 0].astype(f32) + r2[s, h].astype(f32)

    @pl.loop(0, na)
    def _(j):
        s = lax.rem(j + 1, na)
        for h in range(2):
            s1_copy(s, h, 1).wait_recv()
            ref = bit(part, owner(s) + (dy if h else dx), h)
            ref[...] = (ref[...].astype(f32) + r1[s, h, 1].astype(f32)).astype(bf16)
            s2_copy(s, h).start()

        @pl.when(j < out_steps)
        def _():
            p_far(j)

        @pl.when(j >= 1)
        def _():
            for h in range(2):
                bit(part, owner(j), h)[...] = first_sum(j, h).astype(bf16)
            s3_copy(j).start()

    for c in range(na, out_steps):
        p_far(c)

    for h in range(2):
        q_grad[h * piece : (h + 1) * piece, :] = first_sum(0, h)

    def done_copy(c):
        at = pl.ds(pl.multiple_of(c * out_chunk, out_chunk), out_chunk)
        return pltpu.make_async_copy(p_done.at[c], p_out.at[:, at], done_sem.at[c])

    @pl.loop(0, out_steps)
    def _(c):
        kept = dot(p_dir[...], w[back_rows(core, c), :], by_rows)
        p_copy(c).wait_recv()
        p_done[c] = (kept + p_recv[c].astype(f32)).astype(bf16)
        done_copy(c).start()

    @pl.loop(1, n)
    def _(k):
        mh_copy(k, before(k)).wait_recv()

    sums = lax.fori_loop(0, n, lambda i, s: s + mh_slots[i], jnp.zeros((8, tile), f32))
    at = pl.ds(pl.multiple_of(a * tile, tile), tile)
    t_own = lax.fori_loop(
        0, n, lambda i, s: s + t_slots[i, :, at], jnp.zeros((1, tile), f32)
    )
    inv = lax.rsqrt(raw[p_rows : p_rows + 1, at] + raw_far[p_rows : p_rows + 1, at] + 1e-06)
    own_moment, own_hit = sums[0:1, :], sums[1:2, :]
    loss = jnp.log(t_own) - own_hit
    radial = lists[9:10, at] * (own_moment / t_own - own_hit)
    three = jnp.concatenate([loss, inv, inv * radial, jnp.zeros((5, tile), f32)], axis=0)
    turn[...] = jnp.concatenate([three] * (tile // 8), axis=0).T
    mine = turn[pl.ds(pl.multiple_of(b * rows, rows), rows), :]
    loss_ref[...] = pltpu.roll(three, lax.rem(tile - b * rows, tile), 1)[0:1, 0:rows]

    @pl.loop(1, na)
    def _(s):
        s3_copy(s).wait_recv()
        q_grad[...] += r3[s].astype(f32)

    q_dir = (mine[:, 1:2] * (q_grad[...] - q_proj[...] * mine[:, 2:3])).astype(bf16)

    def q_copy(c):
        return remote(q_send.at[c], q_recv.at[c], q_sem.at[0, c], q_sem.at[1, c], other)

    q_chunk = q_send.shape[2]
    q_steps = half // q_chunk

    def q_back(which, c):
        at = pl.ds(pl.multiple_of(which * half + c * q_chunk, q_chunk), q_chunk)
        return dot(q_dir, w[at, :], by_rows)

    for c in range(q_steps):
        q_send[c] = q_back(1 - core, c).astype(bf16)
        q_copy(c).start()
    for c in range(q_steps):
        kept = q_back(core, c)
        q_copy(c).wait_recv()
        q_out[:, c * q_chunk : (c + 1) * q_chunk] = (kept + q_recv[c].astype(f32)).astype(bf16)

    psq_copy.wait_send()
    for c in range(q_steps):
        q_copy(c).wait_send()

    @pl.loop(0, out_steps)
    def _(c):
        p_copy(c).wait_send()
        done_copy(c).wait()

    @pl.loop(1, n)
    def _(k):
        list_copy(k, me).wait_send()
        sq_copy(k, me).wait_send()
        t_copy(k, me).wait_send()
        mh_copy(k, me).wait_send()

    @pl.loop(0, na)
    def _(s):
        for h in range(2):
            first_copy(h, s, column(s)).wait_send()
            then_copy(h, s, 0, column(s)).wait_send()
            then_copy(h, s, 1, column(s) + hop[h][1]).wait_send()
            s1_copy(s, h, 0).wait_send()
            s1_copy(s, h, 1).wait_send()
            s2_copy(s, h).wait_send()

    @pl.loop(1, na)
    def _(s):
        for h in range(2):
            z_copy(h, s, me).wait_send()
        s3_copy(s).wait_send()


def hand_over(loss, q, p, loss_out, q_out, p_out, loss_buf, q_buf, p_buf, sems):
    parts = sems.shape[1] - 2
    size = p.shape[0] // parts
    routes = [(loss, loss_buf, loss_out), (q, q_buf, q_out)]
    for i in range(parts):
        at = slice(i * size, (i + 1) * size)
        routes.append((p.at[at, :], p_buf.at[at, :], p_out.at[at, :]))
    into = [pltpu.make_async_copy(x, y, sems.at[0, i]) for i, (x, y, _) in enumerate(routes)]
    away = [pltpu.make_async_copy(y, z, sems.at[1, i]) for i, (_, y, z) in enumerate(routes)]
    order = list(range(2, parts + 2)) + [0, 1]
    for i in order:
        into[i].start()
    for i in order:
        into[i].wait()
        away[i].start()
    for i in order:
        away[i].wait()


def per_device(
    n, query_states, passage_states, head_weight, positives, negatives, search_cost_incoming_slope
):
    rows, depth = query_states.shape
    p_rows = passage_states.shape[0]
    width = head_weight.shape[1]
    half = depth // 2
    queries = n * rows
    group = tile // rows
    na = n // group
    piece = rows // 2
    names = 1 + negatives.shape[1]
    steps = 4
    dma = pltpu.SemaphoreType.DMA
    vmem = pltpu.VMEM
    flops = 2 * width * (2 * (rows + p_rows) * depth + 3 * queries * p_rows)
    out = pl.pallas_call(
        functools.partial(kernel, n, names),
        out_shape=(
            jax.ShapeDtypeStruct((1, rows), f32),
            jax.ShapeDtypeStruct((rows, half), bf16),
            jax.ShapeDtypeStruct((p_rows, half), bf16),
        ),
        in_specs=[pl.BlockSpec(memory_space=pl.ANY)] * 3
        + [pl.BlockSpec(memory_space=pltpu.VMEM)] * 3,
        out_specs=[pl.BlockSpec(memory_space=pltpu.VMEM)] * 2
        + [pl.BlockSpec(memory_space=pl.ANY)],
        scratch_shapes=[
            vmem((rows, depth), bf16),
            vmem((p_rows, depth), bf16),
            vmem((depth, width), bf16),
            vmem((rows, width), f32),
            vmem((2, queries, width // 2), bf16),
            vmem((p_rows, width), f32),
            vmem((p_rows, width), bf16),
            vmem((p_rows, width), bf16),
            vmem((n, 16, tile), f32),
            vmem((n, 1, tile), f32),
            vmem((16, queries), f32),
            vmem((p_rows, tile), f32),
            vmem((p_rows, tile), f32),
            vmem((p_rows, tile), f32),
            vmem((p_rows + 8, queries), f32),
            vmem((p_rows + 8, queries), f32),
            vmem((p_rows, queries), bf16),
            vmem((p_rows, queries), bf16),
            vmem((n, 1, queries), f32),
            vmem((na, 8, tile), f32),
            vmem((n, 8, tile), f32),
            vmem((tile, tile), f32),
            vmem((queries, width), bf16),
            vmem((na, 2, 2, piece, width), bf16),
            vmem((na, 2, piece, width), bf16),
            vmem((na, rows, width), bf16),
            vmem((rows, width), f32),
            vmem((steps, p_rows, half // steps), bf16),
            vmem((steps, p_rows, half // steps), bf16),
            vmem((2, rows, half // 2), bf16),
            vmem((2, rows, half // 2), bf16),
            vmem((steps, p_rows, half // steps), bf16),
            dma((w_parts + 2,)),
            dma((6,)),
            dma((2, 2)),
            dma((2, 2, na)),
            dma((2, 2, na)),
            dma((2, 2, na, 2)),
            dma((2, n)),
            dma((2, n)),
            dma((2, n)),
            dma((2, n)),
            dma((2, na, 4)),
            dma((2, na, 2)),
            dma((2, na)),
            dma((2, steps)),
            dma((2, 2)),
            dma((steps,)),
        ],
        compiler_params=pltpu.CompilerParams(
            collective_id=0, has_side_effects=True, vmem_limit_bytes=63 * 2**20
        ),
        cost_estimate=pl.CostEstimate(
            flops=flops, bytes_accessed=12 * 2**20, transcendentals=queries * p_rows
        ),
        name="contrastive",
    )(
        query_states,
        passage_states,
        head_weight,
        positives.reshape(1, rows),
        negatives.T,
        search_cost_incoming_slope.reshape(1, rows),
    )
    losses, q_rows, p_rows_out = pl.pallas_call(
        hand_over,
        out_shape=tuple(jax.ShapeDtypeStruct(x.shape, x.dtype) for x in out),
        in_specs=[pl.BlockSpec(memory_space=pl.ANY)] * 3,
        out_specs=[pl.BlockSpec(memory_space=pl.ANY)] * 3,
        scratch_shapes=[vmem(x.shape, x.dtype) for x in out] + [dma((2, 2 + steps))],
        compiler_params=pltpu.CompilerParams(vmem_limit_bytes=60 * 2**20),
        name="hand_over",
    )(*out)
    return losses.reshape(rows), q_rows, p_rows_out


def solution(mesh):
    placed = (P("dp", None), P("dp", None), P(None, "mp"), P("dp"), P("dp", None), P("dp"))
    return jax.shard_map(
        functools.partial(per_device, mesh.shape["dp"]),
        mesh=mesh,
        in_specs=placed,
        out_specs=(P("dp"), P("dp", "mp"), P("dp", "mp")),
        check_vma=False,
    )
```

```python
import functools

import jax
import jax.numpy as jnp
from jax import lax
from jax.experimental import pallas as pl
from jax.experimental.pallas import tpu as pltpu
from jax.sharding import PartitionSpec as P

temperature = 0.02
by_rows = (((1,), (1,)), ((), ()))
by_first = (((0,), (0,)), ((), ()))
f32 = jnp.float32
bf16 = jnp.bfloat16
tile = 128
w_parts = 8
window = 4
strip = 32
s_chunk = 512


def dot(x, y, dims=(((1,), (0,)), ((), ()))):
    return lax.dot_general(x, y, dims, preferred_element_type=f32)


def remote(src, dst, send, recv, where):
    return pltpu.make_async_remote_copy(
        src_ref=src,
        dst_ref=dst,
        send_sem=send,
        recv_sem=recv,
        device_id=where,
        device_id_type=pl.DeviceIdType.MESH,
    )


def kernel(
    n,
    names,
    q_hbm,
    p_hbm,
    w_hbm,
    pos_ref,
    neg_ref,
    slope_ref,
    loss_ref,
    q_out,
    p_out,
    qs,
    ps,
    w,
    q_proj,
    q_all,
    p_proj,
    p_half,
    p_dir,
    list_z,
    list_hop,
    lists,
    psq,
    psq_far,
    col,
    raw,
    raw_far,
    g_q,
    g_p,
    sums_z,
    sums_hop,
    sums_all,
    turn,
    part,
    r1,
    r2,
    r3,
    q_grad,
    p_send,
    p_recv,
    q_send,
    q_recv,
    p_done,
    load,
    pair,
    raw_sem,
    z_sem,
    x_sem,
    y_sem,
    fx_sem,
    fy_sem,
    list_sem,
    sums_sem,
    s1_sem,
    s2_sem,
    s3_sem,
    back_sem,
    q_sem,
    done_sem,
):
    rows, depth = qs.shape
    p_rows, width = p_proj.shape
    queries = q_all.shape[0]
    piece = rows // 2
    group = tile // rows
    na = n // group
    half = depth // 2
    me = lax.axis_index("dp")
    core = lax.axis_index("mp")
    a, b = me // group, lax.rem(me, group)
    x, y = lax.rem(me, 2), lax.rem(me // 2, 2)
    dx, dy = 1 - 2 * x, 2 - 4 * y
    xp, yp, other = {"dp": me + dx}, {"dp": me + dy}, {"mp": 1 - core}

    k_rows = depth // w_parts

    def w_load(i):
        at = pl.ds(pl.multiple_of(i * k_rows, k_rows), k_rows)
        return pltpu.make_async_copy(w_hbm.at[at, :], w.at[at, :], load.at[i])

    q_load = pltpu.make_async_copy(q_hbm, qs, load.at[w_parts])
    p_load = pltpu.make_async_copy(p_hbm, ps, load.at[w_parts + 1])
    q_load.start()
    for i in range(window):
        w_load(i).start()

    barrier = pltpu.get_barrier_semaphore()

    def greet(where):
        pl.semaphore_signal(barrier, inc=1, device_id=where, device_id_type=pl.DeviceIdType.MESH)

    for where in (other, xp, yp):
        greet(where)

    @pl.loop(1, na)
    def _(s):
        greet({"dp": lax.rem(a + s, na) * group + b})

    def hop_copy(hops, sems, k):
        return remote(
            hops.at[2 * k], hops.at[2 * k + 1], sems.at[0, na + k], sems.at[1, na + k], (xp, yp)[k]
        )

    def far_copy(tops, sems, s, i):
        to = {"dp": lax.rem(a + s, na) * group + b}
        return remote(tops.at[i], tops.at[i], sems.at[0, s], sems.at[1, s], to)

    def hop_on(hops, tops, sems, k):
        hop_copy(hops, sems, k).wait_recv()
        if k == 0:
            hops[2] = hops[0] + hops[1]
            hop_copy(hops, sems, 1).start()
        else:
            tops[a] = hops[2] + hops[3]

            @pl.loop(1, na)
            def _(s):
                far_copy(tops, sems, s, a).start()

    def hop_end(tops, sems):
        @pl.loop(1, na)
        def _(s):
            far_copy(tops, sems, s, lax.rem(a - s + na, na)).wait_recv()

    turn[0:24, :] = jnp.zeros((24, tile), f32)
    turn[0 : names - 1, 0:rows] = neg_ref[...].astype(f32)
    turn[8:9, 0:rows] = pos_ref[...].astype(f32)
    turn[16:17, 0:rows] = slope_ref[...]
    neg_lanes, pos_lanes, slope_lanes = [
        pltpu.roll(turn[8 * i : 8 * i + 8, :], b * rows, 1) for i in range(3)
    ]
    lane = lax.broadcasted_iota(jnp.int32, (1, tile), 1)
    mask = lane // rows == b
    list_hop[0] = jnp.concatenate(
        [
            pos_lanes[0:1, :],
            neg_lanes[0 : names - 1, :],
            slope_lanes[0:1, :],
            jnp.zeros((15 - names, tile), f32),
        ],
        axis=0,
    )
    pl.semaphore_wait(barrier, 3 + na - 1)

    q_load.wait()
    total = None
    for i in range(w_parts):
        w_load(i).wait()
        if i + window < w_parts:
            w_load(i + window).start()
        if i + window == w_parts:
            p_load.start()
        at = slice(i * k_rows, (i + 1) * k_rows)
        term = dot(qs[:, at], w[at, :])
        total = term if total is None else total + term
    q_proj[...] = total

    def block(i):
        return q_all.at[pl.ds(pl.multiple_of(i * rows, rows), rows), :]

    def bit(ref, i, h):
        return ref.at[pl.ds(pl.multiple_of(i * rows + h * piece, piece), piece), :]

    q_all[pl.ds(pl.multiple_of(me * rows, rows), rows), :] = q_proj[...].astype(bf16)
    def z_copy(s, i):
        to = {"dp": lax.rem(a + s, na) * group + b}
        return remote(block(i), block(i), z_sem.at[0, s], z_sem.at[1, s], to)

    def column(s):
        return lax.rem(a - s + na, na) * group + b

    def x_copy(s, i):
        return remote(block(i), block(i), x_sem.at[0, s], x_sem.at[1, s], xp)

    def y_copy(s, i):
        return remote(block(i), block(i), y_sem.at[0, s], y_sem.at[1, s], yp)

    def fx_copy(s, i):
        return remote(bit(q_all, i, 1), bit(q_all, i, 1), fx_sem.at[0, s], fx_sem.at[1, s], xp)

    def fy_copy(s, i):
        return remote(bit(q_all, i, 0), bit(q_all, i, 0), fy_sem.at[0, s], fy_sem.at[1, s], yp)

    @pl.loop(1, na)
    def _(s):
        z_copy(s, me).start()

    x_copy(0, me).start()
    y_copy(0, me).start()

    q_square = jnp.sum(q_proj[...] * q_proj[...], axis=1, keepdims=True)
    square_rows = jnp.broadcast_to(q_square, (rows, tile))
    square_lanes = jnp.concatenate([square_rows] * group, axis=0).T
    list_hop[0, names + 1 : names + 2, :] = jnp.where(mask, square_lanes[0:1, :], 0.0)
    hop_copy(list_hop, list_sem, 0).start()

    p_load.wait()
    p_chunk = 256
    p_steps = width // p_chunk
    psq[...] = jnp.zeros_like(psq)
    for j in range(p_steps):
        at = slice(j * p_chunk, (j + 1) * p_chunk)
        out = dot(ps[...], w[:, at])
        p_proj[:, at] = out
        p_half[:, at] = out.astype(bf16)
        psq[...] += jnp.broadcast_to(jnp.sum(out * out, axis=1, keepdims=True), psq.shape)
        lo = 1 + j * (na - 1) // p_steps
        hi = 1 + (j + 1) * (na - 1) // p_steps

        @pl.loop(lo, hi)
        def _(s):
            z_copy(s, column(s)).wait_recv()
            x_copy(s, column(s)).start()
            y_copy(s, column(s)).start()

        if j < 2:
            hop_on(list_hop, list_z, list_sem, j)

    psq_copy = remote(psq, psq_far, pair.at[0], pair.at[1], other)
    psq_copy.start()

    @pl.loop(0, na)
    def _(s):
        x_copy(s, column(s) + dx).wait_recv()
        fy_copy(s, column(s) + dx).start()
        y_copy(s, column(s) + dy).wait_recv()
        fx_copy(s, column(s) + dy).start()

    hop_end(list_z, list_sem)

    @pl.loop(0, na)
    def _(t):
        at = pl.ds(pl.multiple_of(t * tile, tile), tile)
        full = list_z[t]
        lists[:, at] = full
        raw[p_rows : p_rows + 8, at] = jnp.broadcast_to(full[names + 1 : names + 2, :], (8, tile))

    def strip_of(i):
        return pl.ds(pl.multiple_of(i * strip, strip), strip)

    def numbers_of(i):
        first = me * p_rows + i * strip
        return (first + lax.broadcasted_iota(jnp.int32, (strip, 1), 0)).astype(f32)

    def is_own(i):
        return (lists[0:1, :] == numbers_of(i)).astype(f32)

    @pl.loop(0, p_rows // strip)
    def _(i):
        numbers = numbers_of(i)
        named = jnp.sum(is_own(i), axis=1, keepdims=True)
        col[strip_of(i), :] = jnp.broadcast_to(named, (strip, tile))
        times = (lists[1:2, :] == numbers).astype(f32)
        for k in range(2, names):
            times = times + (lists[k : k + 1, :] == numbers).astype(f32)
        g_q[strip_of(i), :] = times.astype(bf16)

    psq_copy.wait_recv()

    @pl.loop(0, na)
    def _(s):
        fx_copy(s, column(s) + dx + dy).wait_recv()
        fy_copy(s, column(s) + dx + dy).wait_recv()

    s_rows = p_rows // 2
    sq_far_copy = remote(
        raw.at[p_rows : p_rows + 8, :], raw_far.at[p_rows : p_rows + 8, :], pair.at[4], pair.at[5], other
    )
    sq_far_copy.start()

    def raw_copy(i):
        at = pl.ds(pl.multiple_of(i * s_rows, s_rows), s_rows)
        return remote(raw.at[at, :], raw_far.at[at, :], raw_sem.at[0, i], raw_sem.at[1, i], other)

    for i in range(2):
        at = slice(i * s_rows, (i + 1) * s_rows)
        for j in range(queries // s_chunk):
            to = slice(j * s_chunk, (j + 1) * s_chunk)
            raw[at, to] = dot(p_half[at, :], q_all[to, :], by_rows)
        raw_copy(i).start()

    sq_far_copy.wait()

    def q_scale():
        return lax.rsqrt(raw[p_rows : p_rows + 1, :] + raw_far[p_rows : p_rows + 1, :] + 1e-06)

    def p_scale(at):
        return lax.rsqrt(psq[at, 0:1] + psq_far[at, 0:1] + 1e-06)

    zero = jnp.zeros((1, queries), f32)

    def score_strip(i, sums):
        at = strip_of(i)
        scores = (raw[at, :] + raw_far[at, :]) * (q_scale() * (1.0 / temperature)) * p_scale(at)
        powers = (col[at, 0:1] + g_q[at, :].astype(f32)) * jnp.exp(scores)
        raw[at, :] = scores
        raw_far[at, :] = powers
        new = (powers, powers * scores, is_own(i) * scores)
        return tuple(s + jnp.sum(v, axis=0, keepdims=True) for s, v in zip(sums, new))

    sums = (zero, zero, zero)
    s_strips = s_rows // strip
    for i in range(2):
        raw_copy(i).wait()
        sums = lax.fori_loop(i * s_strips, (i + 1) * s_strips, score_strip, sums)
    total, moment, hit = sums

    sums_hop[0] = jnp.concatenate([total, moment, hit, zero], axis=0)
    hop_copy(sums_hop, sums_sem, 0).start()
    hop_on(sums_hop, sums_z, sums_sem, 0)
    hop_on(sums_hop, sums_z, sums_sem, 1)
    hop_end(sums_z, sums_sem)
    sums_all[...] = lax.fori_loop(1, na, lambda i, t: t + sums_z[i], sums_z[0])
    total = sums_all[0:1, :]

    @pl.loop(0, p_rows // strip)
    def _(i):
        at = strip_of(i)
        slope = lists[9:10, :] * (1.0 / temperature)
        grads = slope * (raw_far[at, :] * (1.0 / total) - is_own(i))
        g_q[at, :] = (grads * p_scale(at)).astype(bf16)
        g_p[at, :] = (grads * q_scale()).astype(bf16)
        radial = temperature * jnp.sum(grads * raw[at, :], axis=1, keepdims=True)
        col[at, :] = jnp.broadcast_to(radial, (strip, tile))

    def owner(s):
        return lax.rem(a + s, na) * group + b

    def s1_copy(s, h, c):
        i = owner(s) + (dx if h else dy) + (dx + dy - (dx if h else dy)) * c
        return remote(
            bit(part, i, h),
            r1.at[s, h, c],
            s1_sem.at[0, s, 2 * h + c],
            s1_sem.at[1, s, 2 * h + c],
            xp if h else yp,
        )

    def s2_copy(s, h):
        i = owner(s) + (dy if h else dx)
        return remote(
            bit(part, i, h), r2.at[s, h], s2_sem.at[0, s, h], s2_sem.at[1, s, h], yp if h else xp
        )

    def s3_copy(s):
        i = owner(s)
        src = part.at[pl.ds(pl.multiple_of(i * rows, rows), rows), :]
        return remote(src, r3.at[s], s3_sem.at[0, s], s3_sem.at[1, s], {"dp": i})

    @pl.loop(0, na)
    def _(j):
        s = lax.rem(j + 1, na)
        at = pl.ds(pl.multiple_of(lax.rem(a + s, na) * tile, tile), tile)
        part[at, :] = dot(g_q[:, at], p_half[...], by_first).astype(bf16)
        for c in (1, 0):
            for h in range(2):
                s1_copy(s, h, c).start()

    for j in range(p_steps):
        at = slice(j * p_chunk, (j + 1) * p_chunk)
        grad = dot(g_p[...], q_all[:, at])
        inv = p_scale(slice(0, p_rows))
        p_dir[:, at] = (inv * (grad - p_proj[:, at] * (inv * col[:, 0:1]))).astype(bf16)

    out_chunk = p_send.shape[2]
    out_steps = half // out_chunk

    def back_rows(which, c):
        return pl.ds(pl.multiple_of(which * half + c * out_chunk, out_chunk), out_chunk)

    def p_copy(c):
        return remote(p_send.at[c], p_recv.at[c], back_sem.at[0, c], back_sem.at[1, c], other)

    def p_far(c):
        p_send[c] = dot(p_dir[...], w[back_rows(1 - core, c), :], by_rows).astype(bf16)
        p_copy(c).start()

    def first_sum(s, h):
        s1_copy(s, h, 0).wait_recv()
        s2_copy(s, h).wait_recv()
        mine = bit(part, owner(s), h)[...].astype(f32)
        return mine + r1[s, h, 0].astype(f32) + r2[s, h].astype(f32)

    @pl.loop(0, na)
    def _(j):
        s = lax.rem(j + 1, na)
        for h in range(2):
            s1_copy(s, h, 1).wait_recv()
            ref = bit(part, owner(s) + (dy if h else dx), h)
            ref[...] = (ref[...].astype(f32) + r1[s, h, 1].astype(f32)).astype(bf16)
            s2_copy(s, h).start()

        @pl.when(j < out_steps)
        def _():
            p_far(j)

        @pl.when(j >= 1)
        def _():
            for h in range(2):
                bit(part, owner(j), h)[...] = first_sum(j, h).astype(bf16)
            s3_copy(j).start()

    for c in range(na, out_steps):
        p_far(c)

    for h in range(2):
        q_grad[h * piece : (h + 1) * piece, :] = first_sum(0, h)

    def done_copy(c):
        at = pl.ds(pl.multiple_of(c * out_chunk, out_chunk), out_chunk)
        return pltpu.make_async_copy(p_done.at[c], p_out.at[:, at], done_sem.at[c])

    @pl.loop(0, out_steps)
    def _(c):
        kept = dot(p_dir[...], w[back_rows(core, c), :], by_rows)
        p_copy(c).wait_recv()
        p_done[c] = (kept + p_recv[c].astype(f32)).astype(bf16)
        done_copy(c).start()

    at = pl.ds(pl.multiple_of(a * tile, tile), tile)
    t_own, own_moment, own_hit = [sums_all[i : i + 1, at] for i in range(3)]
    inv = lax.rsqrt(raw[p_rows : p_rows + 1, at] + raw_far[p_rows : p_rows + 1, at] + 1e-06)
    loss = jnp.log(t_own) - own_hit
    radial = lists[9:10, at] * (own_moment / t_own - own_hit)
    three = jnp.concatenate([loss, inv, inv * radial, jnp.zeros((5, tile), f32)], axis=0)
    turn[...] = jnp.concatenate([three] * (tile // 8), axis=0).T
    mine = turn[pl.ds(pl.multiple_of(b * rows, rows), rows), :]
    loss_ref[...] = pltpu.roll(three, lax.rem(tile - b * rows, tile), 1)[0:1, 0:rows]

    @pl.loop(1, na)
    def _(s):
        s3_copy(s).wait_recv()
        q_grad[...] += r3[s].astype(f32)

    q_dir = (mine[:, 1:2] * (q_grad[...] - q_proj[...] * mine[:, 2:3])).astype(bf16)

    def q_copy(c):
        return remote(q_send.at[c], q_recv.at[c], q_sem.at[0, c], q_sem.at[1, c], other)

    q_chunk = q_send.shape[2]
    q_steps = half // q_chunk

    def q_back(which, c):
        at = pl.ds(pl.multiple_of(which * half + c * q_chunk, q_chunk), q_chunk)
        return dot(q_dir, w[at, :], by_rows)

    for c in range(q_steps):
        q_send[c] = q_back(1 - core, c).astype(bf16)
        q_copy(c).start()
    for c in range(q_steps):
        kept = q_back(core, c)
        q_copy(c).wait_recv()
        q_out[:, c * q_chunk : (c + 1) * q_chunk] = (kept + q_recv[c].astype(f32)).astype(bf16)

    psq_copy.wait_send()
    for c in range(q_steps):
        q_copy(c).wait_send()

    @pl.loop(0, out_steps)
    def _(c):
        p_copy(c).wait_send()
        done_copy(c).wait()

    for k in range(2):
        hop_copy(list_hop, list_sem, k).wait_send()
        hop_copy(sums_hop, sums_sem, k).wait_send()

    @pl.loop(0, na)
    def _(s):
        x_copy(s, column(s)).wait_send()
        y_copy(s, column(s)).wait_send()
        fy_copy(s, column(s) + dx).wait_send()
        fx_copy(s, column(s) + dy).wait_send()
        for h in range(2):
            s1_copy(s, h, 0).wait_send()
            s1_copy(s, h, 1).wait_send()
            s2_copy(s, h).wait_send()

    @pl.loop(1, na)
    def _(s):
        z_copy(s, me).wait_send()
        far_copy(list_z, list_sem, s, a).wait_send()
        far_copy(sums_z, sums_sem, s, a).wait_send()
        s3_copy(s).wait_send()


def hand_over(loss, q, p, loss_out, q_out, p_out, loss_buf, q_buf, p_buf, sems):
    parts = sems.shape[1] - 2
    size = p.shape[0] // parts
    routes = [(loss, loss_buf, loss_out), (q, q_buf, q_out)]
    for i in range(parts):
        at = slice(i * size, (i + 1) * size)
        routes.append((p.at[at, :], p_buf.at[at, :], p_out.at[at, :]))
    into = [pltpu.make_async_copy(x, y, sems.at[0, i]) for i, (x, y, _) in enumerate(routes)]
    away = [pltpu.make_async_copy(y, z, sems.at[1, i]) for i, (_, y, z) in enumerate(routes)]
    order = list(range(2, parts + 2)) + [0, 1]
    for i in order:
        into[i].start()
    for i in order:
        into[i].wait()
        away[i].start()
    for i in order:
        away[i].wait()


def per_device(
    n, query_states, passage_states, head_weight, positives, negatives, search_cost_incoming_slope
):
    rows, depth = query_states.shape
    p_rows = passage_states.shape[0]
    width = head_weight.shape[1]
    half = depth // 2
    queries = n * rows
    group = tile // rows
    na = n // group
    piece = rows // 2
    names = 1 + negatives.shape[1]
    steps = 4
    dma = pltpu.SemaphoreType.DMA
    vmem = pltpu.VMEM
    flops = 2 * width * (2 * (rows + p_rows) * depth + 3 * queries * p_rows)
    out = pl.pallas_call(
        functools.partial(kernel, n, names),
        out_shape=(
            jax.ShapeDtypeStruct((1, rows), f32),
            jax.ShapeDtypeStruct((rows, half), bf16),
            jax.ShapeDtypeStruct((p_rows, half), bf16),
        ),
        in_specs=[pl.BlockSpec(memory_space=pl.ANY)] * 3
        + [pl.BlockSpec(memory_space=pltpu.VMEM)] * 3,
        out_specs=[pl.BlockSpec(memory_space=pltpu.VMEM)] * 2
        + [pl.BlockSpec(memory_space=pl.ANY)],
        scratch_shapes=[
            vmem((rows, depth), bf16),
            vmem((p_rows, depth), bf16),
            vmem((depth, width), bf16),
            vmem((rows, width), f32),
            vmem((queries, width), bf16),
            vmem((p_rows, width), f32),
            vmem((p_rows, width), bf16),
            vmem((p_rows, width), bf16),
            vmem((na, 16, tile), f32),
            vmem((4, 16, tile), f32),
            vmem((16, queries), f32),
            vmem((p_rows, tile), f32),
            vmem((p_rows, tile), f32),
            vmem((p_rows, tile), f32),
            vmem((p_rows + 8, queries), f32),
            vmem((p_rows + 8, queries), f32),
            vmem((p_rows, queries), bf16),
            vmem((p_rows, queries), bf16),
            vmem((na, 4, queries), f32),
            vmem((4, 4, queries), f32),
            vmem((4, queries), f32),
            vmem((tile, tile), f32),
            vmem((queries, width), bf16),
            vmem((na, 2, 2, piece, width), bf16),
            vmem((na, 2, piece, width), bf16),
            vmem((na, rows, width), bf16),
            vmem((rows, width), f32),
            vmem((steps, p_rows, half // steps), bf16),
            vmem((steps, p_rows, half // steps), bf16),
            vmem((2, rows, half // 2), bf16),
            vmem((2, rows, half // 2), bf16),
            vmem((steps, p_rows, half // steps), bf16),
            dma((w_parts + 2,)),
            dma((6,)),
            dma((2, 2)),
            dma((2, na)),
            dma((2, na)),
            dma((2, na)),
            dma((2, na)),
            dma((2, na)),
            dma((2, na + 2)),
            dma((2, na + 2)),
            dma((2, na, 4)),
            dma((2, na, 2)),
            dma((2, na)),
            dma((2, steps)),
            dma((2, 2)),
            dma((steps,)),
        ],
        compiler_params=pltpu.CompilerParams(
            collective_id=0, has_side_effects=True, vmem_limit_bytes=63 * 2**20
        ),
        cost_estimate=pl.CostEstimate(
            flops=flops, bytes_accessed=12 * 2**20, transcendentals=queries * p_rows
        ),
        name="contrastive",
    )(
        query_states,
        passage_states,
        head_weight,
        positives.reshape(1, rows),
        negatives.T,
        search_cost_incoming_slope.reshape(1, rows),
    )
    losses, q_rows, p_rows_out = pl.pallas_call(
        hand_over,
        out_shape=tuple(jax.ShapeDtypeStruct(x.shape, x.dtype) for x in out),
        in_specs=[pl.BlockSpec(memory_space=pl.ANY)] * 3,
        out_specs=[pl.BlockSpec(memory_space=pl.ANY)] * 3,
        scratch_shapes=[vmem(x.shape, x.dtype) for x in out] + [dma((2, 2 + steps))],
        compiler_params=pltpu.CompilerParams(vmem_limit_bytes=60 * 2**20),
        name="hand_over",
    )(*out)
    return losses.reshape(rows), q_rows, p_rows_out


def solution(mesh):
    placed = (P("dp", None), P("dp", None), P(None, "mp"), P("dp"), P("dp", None), P("dp"))
    return jax.shard_map(
        functools.partial(per_device, mesh.shape["dp"]),
        mesh=mesh,
        in_specs=placed,
        out_specs=(P("dp"), P("dp", "mp"), P("dp", "mp")),
        check_vma=False,
    )
```
